512 devices in a mesh: group: 32 (over z, core), member: 16 (over x, y).
Axes of the slice: x: 4, y: 4, z: 16, core: 2. Of those that a mesh axis runs over, the one named last changes fastest.
Arguments:
- rhs: bfloat16 [32, 16, 768, 128], P('group', 'member'), may hold values from -6 to 6
- leaf_pivot_inverse: bfloat16 [32, 16, 768, 768], P('group', 'member'), may hold values from -1.5 to 1.5, as said below
- leaf_border_block: bfloat16 [32, 16, 512, 768], P('group', 'member'), may hold values from -0.21875 to 0.21875
- leaf_map: int32 [32, 16, 4], P('group'), may hold values from 0 to 47, as said below
- mid_inverse: bfloat16 [32, 2048, 2048], P('group', 'member'), may hold values from -1.5 to 1.5, as said below
- mid_border: bfloat16 [32, 4096, 2048], P('group', None, 'member'), may hold values from -0.125 to 0.125
- root_map: int32 [32, 16, 2], P('group', 'member'), may hold values from 0 to 3, as said below
- root_inverse: bfloat16 [8192, 8192], P('group', 'member'), may hold values from -0.5 to 0.5, as said below
Outputs:
- leaf_solution: bfloat16 [32, 16, 768, 128], P('group', 'member')
- mid_solution: bfloat16 [32, 2048, 128], P('group', 'member')
- root_solution: bfloat16 [16, 512, 128], P('member', 'group')
The draws below stay inside these ranges and needn't reach their ends.
Inputs may be any that keep to these rules, and one draw needn't show every extreme that they name: `leaf_map`: for each (g, m) the 4 entries are distinct; a value k below 16 names pivot block k of the mid-level front, a larger one border block k - 16. `root_map`: for each (g, m) the entries are distinct. `leaf_pivot_inverse`: each [768, 768] matrix is lower triangular with a positive diagonal, as the inverse of a Cholesky factor is: every entry above the diagonal is zero. `mid_inverse`: each [2048, 2048] matrix is lower triangular with a positive diagonal, as the inverse of a Cholesky factor is: every entry above the diagonal is zero. `root_inverse`: lower triangular with a positive diagonal, as the inverse of a Cholesky factor is: every entry above the diagonal is zero.
All inputs are finite; a program needn't handle non-finite values.
Results may differ from the reference program's by a relative error of at most 0.028.
Values may be sent and summed in bfloat16 or wider, within the bound.
A program may use at most 64 MiB of HBM per device.

```python
import math
import jax
import jax.numpy as jnp
from jax import lax

P0 = 768
B0 = 512
P1 = 2048
B1 = 4096
ROOT = 8192
BLOCK = 128
R = 128
GROUPS = 32
MEMBERS = 16


def lower_factor(key, amount, size_order, scale_level):
    row_ids = lax.broadcasted_iota(jnp.int32, (size_order, size_order), 0)
    col_ids = lax.broadcasted_iota(jnp.int32, (size_order, size_order), 1)

    def one_factor(front_count):
        subkey = jax.random.fold_in(key, front_count)
        key_lower, key_diagonal = jax.random.split(subkey)
        values = jnp.clip(jax.random.normal(key_lower, (size_order, size_order), jnp.float32), -4.0, 4.0)
        diagonal = jax.random.uniform(key_diagonal, (size_order,), jnp.float32, 0.6, 1.4)
        lower_part = jnp.where(row_ids > col_ids, values * (0.9 / math.sqrt(size_order)), 0.0)
        return scale_level * (lower_part + jnp.where(row_ids == col_ids, diagonal[:, None], 0.0))
    return lax.map(one_factor, jnp.arange(amount, dtype=jnp.int32))


def distinct_picks(key, amount, pool_size, picked_count):
    scores = jax.random.randint(key, (amount, pool_size), 0, 1 << 20, jnp.int32) * pool_size
    scores = scores + lax.broadcasted_iota(jnp.int32, (amount, pool_size), 1)
    ranking = jnp.argsort(scores, axis=1, stable=True)
    return ranking[:, :picked_count].astype(jnp.int32)


def draw_leaf_pivot_inverse(key, part):
    factor = lower_factor(jax.random.fold_in(key, 1), GROUPS * MEMBERS, P0, 1.0)
    return factor.reshape(GROUPS, MEMBERS, P0, P0).astype(jnp.bfloat16)


def draw_mid_inverse(key, part):
    factor = lower_factor(jax.random.fold_in(key, 2), GROUPS, P1, 0.7)
    return factor.astype(jnp.bfloat16)


def draw_root_inverse(key, part):
    factor = lower_factor(jax.random.fold_in(key, 3), 1, ROOT, 0.25)
    return factor.reshape(ROOT, ROOT).astype(jnp.bfloat16)


def draw_leaf_map(key, part):
    picks = distinct_picks(jax.random.fold_in(key, 11), GROUPS * MEMBERS, P1 // BLOCK + B1 // BLOCK, B0 // BLOCK)
    return picks.reshape(GROUPS, MEMBERS, B0 // BLOCK)


def draw_root_map(key, part):
    picks = distinct_picks(jax.random.fold_in(key, 12), GROUPS * MEMBERS, ROOT // (BLOCK * MEMBERS), B1 // (BLOCK * MEMBERS))
    return picks.reshape(GROUPS, MEMBERS, B1 // (BLOCK * MEMBERS))


def level_of(rng, extent, pieces, low, high):
    def one(axis_at, shards_of):
        heights = jax.random.uniform(jax.random.fold_in(jax.random.fold_in(rng, 6), axis_at), (shards_of,), jnp.float32, low / len(pieces), high / len(pieces))
        return jnp.repeat(jnp.exp(heights), extent[axis_at] // shards_of).reshape((-1,) + (1,) * (len(extent) - axis_at - 1))

    factor_of = one(*pieces[0])
    for cut in pieces[1:]:
        factor_of = factor_of * one(*cut)
    return factor_of


def noise(rng, extent, deviation, bound, pieces=(), kind=jnp.bfloat16):
    gain = level_of(rng, extent, pieces, -0.22, 0.18) if pieces else 1.0
    drawn = jax.random.normal(rng, extent, jnp.float32) * deviation * gain
    return jnp.minimum(jnp.maximum(drawn, -bound), bound).astype(kind)


def setup_inputs(seed: int = 0) -> dict:
    key_of = jax.random.split(jax.random.key(seed), 9)
    return {
        "rhs": noise(key_of[0], (GROUPS, MEMBERS, P0, R), 1.0, 6.0, ((0, 32), (1, 16))),
        "leaf_pivot_inverse": draw_leaf_pivot_inverse(jax.random.fold_in(key_of[8], 71), 0),
        "leaf_border_block": noise(key_of[2], (GROUPS, MEMBERS, B0, P0), P0 ** -0.5, 0.21875, ((0, 32), (1, 16))),
        "leaf_map": draw_leaf_map(jax.random.fold_in(key_of[8], 71), 0),
        "mid_inverse": draw_mid_inverse(jax.random.fold_in(key_of[8], 71), 0),
        "mid_border": noise(key_of[5], (GROUPS, B1, P1), P1 ** -0.5, 0.125, ((0, 32), (2, 16))),
        "root_map": draw_root_map(jax.random.fold_in(key_of[8], 71), 0),
        "root_inverse": draw_root_inverse(jax.random.fold_in(key_of[8], 71), 0),
    }


def place_blocks(block_ids, targets, source_terms):
    selection_mask = (block_ids[:, None] == targets[None, :]).astype(jnp.float32)
    return jnp.einsum("ng,gcy->ncy", selection_mask, source_terms.astype(jnp.float32), precision=lax.Precision.HIGHEST)


def reference(rhs, leaf_pivot_inverse, leaf_border_block, leaf_map, mid_inverse, mid_border, root_map, root_inverse):
    groups = rhs.shape[0]
    members = rhs.shape[1]
    columns = rhs.shape[3]
    pivot_blocks = P1 // BLOCK
    front_blocks = pivot_blocks + B1 // BLOCK
    leaf_blocks = B0 // BLOCK
    per_member = B1 // (BLOCK * members)
    root_per = ROOT // (BLOCK * members)
    all_blocks = jnp.arange(front_blocks, dtype=jnp.int32)

    def forward_group(front_count):
        leaf_cholesky_factor = leaf_pivot_inverse[front_count].astype(jnp.float32)
        leaf_forward_solve = jnp.einsum("luc,lcd->lud", leaf_cholesky_factor, rhs[front_count].astype(jnp.float32)).astype(jnp.bfloat16)
        leaf_output = (-jnp.einsum("luc,lcd->lud", leaf_border_block[front_count].astype(jnp.float32), leaf_forward_solve.astype(jnp.float32))).astype(jnp.bfloat16)
        targets = leaf_map[front_count].reshape(members * leaf_blocks)
        front = place_blocks(all_blocks, targets, leaf_output.reshape(members * leaf_blocks, BLOCK, columns))
        front = front.reshape(front_blocks * BLOCK, columns)
        mid_rhs = front[:P1].astype(jnp.bfloat16)
        mid_forward = jnp.dot(mid_inverse[front_count], mid_rhs, preferred_element_type=jnp.float32).astype(jnp.bfloat16)
        mid_update = front[P1:] - jnp.dot(mid_border[front_count], mid_forward, preferred_element_type=jnp.float32)
        return leaf_forward_solve, mid_forward, mid_update

    leaf_forward_solve, mid_forward, mid_update = lax.map(forward_group, jnp.arange(groups, dtype=jnp.int32))
    chooser = (root_map[..., None] == jnp.arange(root_per, dtype=jnp.int32)).astype(jnp.float32)
    border_blocks = mid_update.reshape(groups, members, per_member, BLOCK * columns)
    root_rhs = jnp.einsum("gmiq,gmix->mqx", chooser, border_blocks, precision=lax.Precision.HIGHEST)
    root_rhs = root_rhs.reshape(ROOT, columns).astype(jnp.bfloat16)
    root_forward = jnp.dot(root_inverse, root_rhs, preferred_element_type=jnp.float32).astype(jnp.bfloat16)
    root_values = jnp.dot(root_inverse.T, root_forward, preferred_element_type=jnp.float32).astype(jnp.bfloat16)
    root_blocks = root_values.reshape(members, root_per, BLOCK * columns).astype(jnp.float32)
    border_values = jnp.einsum("gmiq,mqx->gmix", chooser, root_blocks, precision=lax.Precision.HIGHEST)
    border_values = border_values.astype(jnp.bfloat16).reshape(groups, B1, columns)

    def backward_group(front_count):
        border_here = border_values[front_count]
        mid_back = (mid_forward[front_count].astype(jnp.float32) - jnp.dot(mid_border[front_count].T, border_here, preferred_element_type=jnp.float32)).astype(jnp.bfloat16)
        inverse_row_set = mid_inverse[front_count].reshape(members, P1 // members, P1).astype(jnp.float32)
        backward_row_set = mid_back.reshape(members, P1 // members, columns).astype(jnp.float32)
        partial_value_rows = jnp.einsum("gxa,gxu->gau", inverse_row_set, backward_row_set).astype(jnp.bfloat16)
        mid_values = jnp.sum(partial_value_rows.astype(jnp.float32), axis=0).astype(jnp.bfloat16)
        front_values = jnp.concatenate([mid_values, border_here], axis=0).reshape(front_blocks, BLOCK, columns)
        targets = leaf_map[front_count].reshape(members * leaf_blocks)
        selected_items = place_blocks(targets, all_blocks, front_values).astype(jnp.bfloat16).reshape(members, B0, columns)
        leaf_backward_solve = (leaf_forward_solve[front_count].astype(jnp.float32) - jnp.einsum("aun,aue->ane", leaf_border_block[front_count].astype(jnp.float32), selected_items.astype(jnp.float32))).astype(jnp.bfloat16)
        leaf_value_rows = jnp.einsum("aun,aue->ane", leaf_pivot_inverse[front_count].astype(jnp.float32), leaf_backward_solve.astype(jnp.float32)).astype(jnp.bfloat16)
        return leaf_value_rows, mid_values

    leaf_solution, mid_solution = lax.map(backward_group, jnp.arange(groups, dtype=jnp.int32))
    return leaf_solution, mid_solution, root_values.reshape(members, ROOT // members, columns)
```

```python
import functools

import jax
import jax.numpy as jnp
from jax import lax
from jax.experimental import pallas as pl
from jax.experimental.pallas import tpu as pltpu
from jax.sharding import PartitionSpec as P

BLOCK = 128
SIDE = 4
MEMBERS = 16
CORES = 2
CHIPS = 16
GROUPS = 32
LEAF = 768
EDGE = 512
LEAF_BLOCKS = EDGE // BLOCK
PIVOTS = 2048
PIVOT_BLOCKS = PIVOTS // BLOCK
BORDER = 4096
FRONT_BLOCKS = (PIVOTS + BORDER) // BLOCK
SHARE = 512
ROOT_ROWS = 256
PIECE = 16
MESH = pl.DeviceIdType.MESH
F32 = jnp.float32
BF16 = jnp.bfloat16

MEMBER_OFFSETS = [(a, b) for a in range(SIDE) for b in range(SIDE) if a or b]
GROUP_OFFSETS = sorted(
    [(a, b) for a in range(CHIPS) for b in range(CORES) if a or b],
    key=lambda o: -min(o[0], CHIPS - o[0]),
)


def dot(a, b):
    return jnp.dot(a, b, preferred_element_type=F32)


def whole_kernel(
    rhs,
    leaf_inverse,
    leaf_edge,
    leaf_map,
    mid_inverse,
    mid_border,
    root_map,
    root_inverse,
    leaf_o,
    mid_o,
    root_o,
    v_rhs,
    v_leaf,
    v_edge,
    v_mid,
    v_border,
    v_root,
    t_leaf,
    t_edge,
    t_mid,
    t_border,
    t_root,
    forward,
    leaf_out,
    s1,
    r1,
    s2,
    r2,
    mid_forward,
    s3,
    r3,
    update,
    s4,
    r4,
    s4b,
    b_root,
    s5,
    r5,
    s5b,
    y_root,
    s6,
    r6,
    s6b,
    x_root,
    front,
    mid_back,
    s8,
    r8,
    load_sems,
    send_sems,
    m1,
    m2,
    m3,
    m5,
    m5b,
    m7,
    m8,
    m8b,
    g_sems,
):
    g = lax.axis_index("group")
    m = lax.axis_index("member")
    mx, my = m // SIDE, lax.rem(m, SIDE)
    gz, gc = g // CORES, lax.rem(g, CORES)
    members = [lax.rem(mx + a, SIDE) * SIDE + lax.rem(my + b, SIDE) for a, b in MEMBER_OFFSETS]
    groups = [lax.rem(gz + a, CHIPS) * CORES + lax.rem(gc + b, CORES) for a, b in GROUP_OFFSETS]

    barrier = pltpu.get_barrier_semaphore()
    for d in groups:
        pl.semaphore_signal(barrier, inc=1, device_id=(d, m), device_id_type=MESH)
    for d in members:
        pl.semaphore_signal(barrier, inc=1, device_id=(g, d), device_id_type=MESH)

    loads = []
    for i, (src, dst) in enumerate(
        [
            (rhs.at[0, 0], v_rhs),
            (leaf_inverse.at[0, 0], v_leaf),
            (leaf_edge.at[0, 0], v_edge),
            (mid_inverse.at[0], v_mid),
            (mid_border.at[0], v_border),
            (root_inverse, v_root),
        ]
    ):
        c = pltpu.make_async_copy(src, dst, load_sems.at[i])
        c.start()
        loads.append(c)

    def send(src, dst, ssem, rsem, device):
        c = pltpu.make_async_remote_copy(
            src_ref=src,
            dst_ref=dst,
            send_sem=ssem,
            recv_sem=rsem,
            device_id=device,
            device_id_type=MESH,
        )
        c.start()
        return c

    def drain(ref, sem):
        pltpu.make_async_copy(ref, ref, sem).wait()

    targets = [leaf_map[0, m, j] for j in range(LEAF_BLOCKS)]

    def leaf_block(k):
        idx = jnp.int32(LEAF_BLOCKS)
        for j in range(LEAF_BLOCKS):
            idx = jnp.where(targets[j] == k, j, idx)
        return leaf_out[idx]

    leaf_out[LEAF_BLOCKS] = jnp.zeros((BLOCK, BLOCK), BF16)
    loads[0].wait()
    loads[1].wait()
    for i in range(3):
        rows = pl.ds(i * 256, 256)
        depth = (i + 1) * 256
        forward[rows, :] = dot(v_leaf[rows, :depth], v_rhs[:depth, :]).astype(BF16)
    loads[2].wait()
    for j in range(LEAF_BLOCKS):
        leaf_out[j] = (-dot(v_edge[pl.ds(j * BLOCK, BLOCK), :], forward[...])).astype(BF16)

    pl.semaphore_wait(barrier, len(groups) + len(members))

    c1 = []
    for i, d in enumerate(members):
        s1[i] = leaf_block(d)
        c1.append(send(s1.at[i], r1.at[i], send_sems.at[0], m1.at[i], (g, d)))
    loads[3].wait()
    loads[4].wait()
    total = leaf_block(m).astype(F32)
    for i, c in enumerate(c1):
        c.wait_recv()
        total = total + r1[i].astype(F32)
    s2[...] = total.astype(BF16)
    c2 = []
    for i, d in enumerate(members):
        c2.append(send(s2, r2.at[m], send_sems.at[1], m2.at[i], (g, d)))
    r2[m] = s2[...]
    for c in c2:
        c.wait_recv()
    mf = dot(v_mid[...], r2[...].reshape(PIVOTS, BLOCK)).astype(BF16)
    mid_forward[...] = mf

    def border_term(d, b):
        rows = pl.ds(pl.multiple_of(d * 256 + b * BLOCK, BLOCK), BLOCK)
        return leaf_block(PIVOT_BLOCKS + 2 * d + b).astype(F32) - dot(v_border[rows, :], mid_forward[...])

    c3 = []
    for i, d in enumerate(members):
        for b in range(2):
            s3[i, b] = border_term(d, b).astype(BF16)
        c3.append(send(s3.at[i], r3.at[i], send_sems.at[2], m3.at[i], (g, d)))
    own = [border_term(m, b) for b in range(2)]
    for b in range(2):
        update[b] = own[b]
    loads[5].wait()
    for k in range(4):
        for q in range(2):
            t_root[pl.ds(k * BLOCK, BLOCK), pl.ds(q * BLOCK, BLOCK)] = v_root[
                pl.ds(q * BLOCK, BLOCK), pl.ds(k * BLOCK, BLOCK)
            ].T
    for i, c in enumerate(c3):
        c.wait_recv()
        for b in range(2):
            update[b] = update[b] + r3[i, b].astype(F32)
    update[2] = jnp.zeros((BLOCK, BLOCK), F32)

    picks = [root_map[0, 0, i] for i in range(2)]
    for q in range(4):
        idx = jnp.where(picks[0] == q, 0, jnp.where(picks[1] == q, 1, 2))
        s4[pl.ds(q * BLOCK, BLOCK), :] = update[idx].astype(BF16)

    def sum_over_groups(s, r, ssem, rsem):
        for i, d in enumerate(groups):
            rows = pl.ds(pl.multiple_of(d * PIECE, PIECE), PIECE)
            send(s.at[rows], r.at[i], ssem, rsem, (d, m))

    def finish_groups(s, r, rsem):
        drain(r, rsem)
        acc = s[pl.ds(pl.multiple_of(g * PIECE, PIECE), PIECE), :].astype(F32)
        for i in range(len(groups)):
            acc = acc + r[i].astype(F32)
        return acc.astype(BF16)

    def gather_groups(s, r, ssem, rsem):
        rows = pl.ds(pl.multiple_of(g * PIECE, PIECE), PIECE)
        for i, d in enumerate(groups):
            send(s, r.at[rows], ssem, rsem, (d, m))
        r[rows, :] = s[...]

    sum_over_groups(s4, r4, send_sems.at[3], g_sems.at[0])
    for k in range(PIVOT_BLOCKS):
        t_mid[pl.ds(k * BLOCK, BLOCK), :] = v_mid[:, pl.ds(k * BLOCK, BLOCK)].T
    s4b[...] = finish_groups(s4, r4, g_sems.at[0])
    gather_groups(s4b, b_root, send_sems.at[4], g_sems.at[1])
    for k in range(BORDER // BLOCK):
        t_border[:, pl.ds(k * BLOCK, BLOCK)] = v_border[pl.ds(k * BLOCK, BLOCK), :].T
    drain(r4, g_sems.at[1])

    s5[...] = dot(v_root[...], b_root[...]).astype(BF16)
    c5 = []
    for i, d in enumerate(members):
        rows = pl.ds(pl.multiple_of(d * PIECE, PIECE), PIECE)
        c5.append(send(s5.at[rows], r5.at[i], send_sems.at[5], m5, (g, d)))
    drain(r5, m5)
    rows = pl.ds(pl.multiple_of(m * PIECE, PIECE), PIECE)
    acc = s5[rows, :].astype(F32)
    for i in range(len(members)):
        acc = acc + r5[i].astype(F32)
    s5b[...] = acc.astype(BF16)
    for i, d in enumerate(members):
        send(s5b, y_root.at[rows], send_sems.at[6], m5b, (g, d))
    y_root[rows, :] = s5b[...]
    drain(r5, m5b)

    s6[...] = dot(t_root[...], y_root[...]).astype(BF16)
    sum_over_groups(s6, r6, send_sems.at[7], g_sems.at[2])
    for k in range(LEAF // BLOCK):
        for q in range(EDGE // BLOCK):
            t_edge[pl.ds(k * BLOCK, BLOCK), pl.ds(q * BLOCK, BLOCK)] = v_edge[
                pl.ds(q * BLOCK, BLOCK), pl.ds(k * BLOCK, BLOCK)
            ].T
    s6b[...] = finish_groups(s6, r6, g_sems.at[2])
    root_o[0] = s6b[...]
    x_rows = pl.ds(pl.multiple_of(lax.rem(g, 8) * PIECE, PIECE), PIECE)
    for i, d in enumerate(groups):
        send(s6b, x_root.at[g // 8, x_rows], send_sems.at[8], g_sems.at[3], (d, m))
    x_root[g // 8, x_rows, :] = s6b[...]
    for k in range(LEAF // BLOCK):
        for q in range(k, LEAF // BLOCK):
            t_leaf[pl.ds(k * BLOCK, BLOCK), pl.ds(q * BLOCK, BLOCK)] = v_leaf[
                pl.ds(q * BLOCK, BLOCK), pl.ds(k * BLOCK, BLOCK)
            ].T
        for q in range(k - k % 2, k):
            t_leaf[pl.ds(k * BLOCK, BLOCK), pl.ds(q * BLOCK, BLOCK)] = v_leaf[
                pl.ds(q * BLOCK, BLOCK), pl.ds(k * BLOCK, BLOCK)
            ].T
    drain(r6, g_sems.at[3])

    mine = pl.ds(PIVOT_BLOCKS + 2 * m, 2)
    for i in range(2):
        front[PIVOT_BLOCKS + 2 * m + i] = x_root[picks[i]]
    c7 = []
    for i, d in enumerate(members):
        c7.append(send(front.at[mine], front.at[mine], send_sems.at[9], m7.at[i], (g, d)))
    for c in c7:
        c.wait_recv()
    back = dot(t_border[...], front[PIVOT_BLOCKS:].reshape(BORDER, BLOCK))
    mid_back[...] = (mid_forward[...].astype(F32) - back).astype(BF16)

    def mid_term(d):
        rows = pl.ds(pl.multiple_of(d * BLOCK, BLOCK), BLOCK)
        return dot(t_mid[rows, :], mid_back[...])

    c8 = []
    for i, d in enumerate(members):
        s8[i] = mid_term(d).astype(BF16)
        c8.append(send(s8.at[i], r8.at[i], send_sems.at[10], m8.at[i], (g, d)))
    total = mid_term(m)
    for i, c in enumerate(c8):
        c.wait_recv()
        total = total + r8[i].astype(F32)
    front[m] = total.astype(BF16)
    mid_o[0] = total.astype(BF16)
    c8b = []
    for i, d in enumerate(members):
        c8b.append(send(front.at[m], front.at[m], send_sems.at[11], m8b.at[i], (g, d)))
    for c in c8b:
        c.wait_recv()

    lb = forward[...].astype(F32)
    for j in range(LEAF_BLOCKS):
        lb = lb - dot(t_edge[:, pl.ds(j * BLOCK, BLOCK)], front[targets[j]])
    lb = lb.astype(BF16)
    for i in range(3):
        leaf_o[0, 0, pl.ds(i * 256, 256), :] = dot(
            t_leaf[pl.ds(i * 256, 256), i * 256 :], lb[i * 256 :]
        ).astype(BF16)

    for i, ref in enumerate([s1, s1, s3, r4, r4, r5, r5, r4, r4, s3, s1, s1]):
        drain(ref, send_sems.at[i])


def on_device(*args):
    n_m, n_g = MEMBERS - 1, GROUPS - 1
    dma = pltpu.SemaphoreType.DMA
    block = (BLOCK, BLOCK)
    v = lambda *shape: pltpu.VMEM(shape, BF16)
    scratch = [
        v(LEAF, BLOCK),
        v(LEAF, LEAF),
        v(EDGE, LEAF),
        v(BLOCK, PIVOTS),
        v(BORDER, BLOCK),
        v(ROOT_ROWS, SHARE),
        v(LEAF, LEAF),
        v(LEAF, EDGE),
        v(PIVOTS, BLOCK),
        v(BLOCK, BORDER),
        v(SHARE, ROOT_ROWS),
        v(LEAF, BLOCK),
        v(LEAF_BLOCKS + 1, *block),
        v(n_m, *block),
        v(n_m, *block),
        v(*block),
        v(MEMBERS, *block),
        v(*block),
        v(n_m, 2, *block),
        v(n_m, 2, *block),
        pltpu.VMEM((3, *block), F32),
        v(SHARE, BLOCK),
        v(n_g, PIECE, BLOCK),
        v(PIECE, BLOCK),
        v(SHARE, BLOCK),
        v(ROOT_ROWS, BLOCK),
        v(n_m, PIECE, BLOCK),
        v(PIECE, BLOCK),
        v(ROOT_ROWS, BLOCK),
        v(SHARE, BLOCK),
        v(n_g, PIECE, BLOCK),
        v(PIECE, BLOCK),
        v(4, *block),
        v(FRONT_BLOCKS, *block),
        v(*block),
        v(n_m, *block),
        v(n_m, *block),
        dma((6,)),
        dma((12,)),
        dma((n_m,)),
        dma((n_m,)),
        dma((n_m,)),
        dma,
        dma,
        dma((n_m,)),
        dma((n_m,)),
        dma((n_m,)),
        dma((4,)),
    ]
    anywhere = pl.BlockSpec(memory_space=pl.ANY)
    scalars = pl.BlockSpec(memory_space=pltpu.SMEM)
    vmem = pl.BlockSpec(memory_space=pltpu.VMEM)
    return pl.pallas_call(
        whole_kernel,
        out_shape=(
            jax.ShapeDtypeStruct((1, 1, LEAF, BLOCK), BF16),
            jax.ShapeDtypeStruct((1, BLOCK, BLOCK), BF16),
            jax.ShapeDtypeStruct((1, PIECE, BLOCK), BF16),
        ),
        in_specs=[anywhere, anywhere, anywhere, scalars, anywhere, anywhere, scalars, anywhere],
        out_specs=(vmem, vmem, vmem),
        scratch_shapes=scratch,
        name="solve",
        compiler_params=pltpu.CompilerParams(
            collective_id=0, has_side_effects=True, vmem_limit_bytes=48 * 1024 * 1024
        ),
    )(*args)


def solution(mesh):
    in_specs = (
        P("group", "member", None, None),
        P("group", "member", None, None),
        P("group", "member", None, None),
        P("group", None, None),
        P("group", "member", None),
        P("group", None, "member"),
        P("group", "member", None),
        P("group", "member"),
    )
    out_specs = (
        P("group", "member", None, None),
        P("group", "member", None),
        P("member", "group", None),
    )
    return jax.shard_map(
        on_device, mesh=mesh, in_specs=in_specs, out_specs=out_specs, check_vma=False
    )
```

```python
import functools

import jax
import jax.numpy as jnp
from jax import lax
from jax.experimental import pallas as pl
from jax.experimental.pallas import tpu as pltpu
from jax.sharding import PartitionSpec as P

BLOCK = 128
SIDE = 4
MEMBERS = 16
CORES = 2
CHIPS = 16
LEAF = 768
EDGE = 512
LEAF_BLOCKS = EDGE // BLOCK
PIVOTS = 2048
PIVOT_BLOCKS = PIVOTS // BLOCK
BORDER = 4096
FRONT_BLOCKS = (PIVOTS + BORDER) // BLOCK
SHARE = 512
ROOT_ROWS = 256
PIECE = 16
MESH = pl.DeviceIdType.MESH
F32 = jnp.float32
BF16 = jnp.bfloat16

MEMBER_OFFSETS = [
    (2, 2),
    (2, 1),
    (1, 2),
    (2, 3),
    (3, 2),
    (1, 1),
    (3, 3),
    (1, 3),
    (3, 1),
    (2, 0),
    (0, 2),
    (1, 0),
    (3, 0),
    (0, 1),
    (0, 3),
]
CHIP_OFFSETS = sorted(range(1, CHIPS), key=lambda a: -min(a, CHIPS - a))
NEAR = (2, 1, 3)


def dot(a, b):
    return jnp.dot(a, b, preferred_element_type=F32)


def whole_kernel(
    rhs,
    leaf_inverse,
    leaf_edge,
    leaf_map,
    mid_inverse,
    mid_border,
    root_map,
    root_inverse,
    leaf_o,
    mid_o,
    root_o,
    v_rhs,
    v_leaf,
    v_edge,
    v_mid,
    v_border,
    v_root,
    t_leaf,
    t_edge,
    t_mid,
    t_border,
    t_root,
    forward,
    leaf_out,
    s1,
    r1,
    s2,
    r2,
    mid_forward,
    s3,
    r3,
    line,
    u3,
    w3,
    update,
    s4,
    p4,
    u4,
    r4,
    b_root,
    s5,
    r5,
    s5b,
    y_root,
    s6,
    p6,
    u6,
    r6,
    x_root,
    x_blocks,
    front,
    mid_back,
    s8,
    r8,
    load_sems,
    send_sems,
    m1,
    t2,
    m2,
    t3,
    m3,
    t3b,
    m3b,
    m5,
    m5b,
    t7,
    m7,
    t8,
    m8,
    m8b,
    g_sems,
    pair_sems,
):
    g = lax.axis_index("group")
    m = lax.axis_index("member")
    mx, my = m // SIDE, lax.rem(m, SIDE)
    gz, gc = g // CORES, lax.rem(g, CORES)
    other = gz * CORES + 1 - gc

    def member_at(a, b):
        return lax.rem(mx + a, SIDE) * SIDE + lax.rem(my + b, SIDE)

    members, sources = [], []
    for a, b in MEMBER_OFFSETS:
        up, down = member_at(a, b), member_at((SIDE - a) % SIDE, (SIDE - b) % SIDE)
        members.append(jnp.where(gc == 0, up, down))
        sources.append(jnp.where(gc == 0, down, up))
    chips = [lax.rem(gz + a, CHIPS) for a in CHIP_OFFSETS]

    barrier = pltpu.get_barrier_semaphore()
    for z in chips:
        pl.semaphore_signal(barrier, inc=1, device_id=(z * CORES + gc, m), device_id_type=MESH)
    pl.semaphore_signal(barrier, inc=1, device_id=(other, m), device_id_type=MESH)
    for d in members:
        pl.semaphore_signal(barrier, inc=1, device_id=(g, d), device_id_type=MESH)

    loads = []
    for i, (src, dst) in enumerate(
        [
            (rhs.at[0, 0], v_rhs),
            (leaf_inverse.at[0, 0], v_leaf),
            (leaf_edge.at[0, 0], v_edge),
            (mid_inverse.at[0], v_mid),
            (mid_border.at[0], v_border),
            (root_inverse, v_root),
        ]
    ):
        c = pltpu.make_async_copy(src, dst, load_sems.at[i])
        c.start()
        loads.append(c)

    def copy_to(src, dst, ssem, rsem, device):
        return pltpu.make_async_remote_copy(
            src_ref=src,
            dst_ref=dst,
            send_sem=ssem,
            recv_sem=rsem,
            device_id=device,
            device_id_type=MESH,
        )

    def send(*args):
        c = copy_to(*args)
        c.start()
        return c

    def drain(ref, sem):
        pltpu.make_async_copy(ref, ref, sem).wait()

    sent = []
    partial_sends = []
    sent_copies = []
    pending = list(loads)

    def loaded(n):
        for _ in range(n):
            pending.pop(0).wait()

    def finish():
        loaded(len(pending))
        for ref, i in sent:
            drain(ref, i)
        for when, c in partial_sends:
            pl.when(when)(c.wait_send)
        for c in sent_copies:
            c.wait_send()

    targets = [leaf_map[0, j, m] for j in range(LEAF_BLOCKS)]

    def leaf_block(k):
        idx = jnp.int32(LEAF_BLOCKS)
        for j in range(LEAF_BLOCKS):
            idx = jnp.where(targets[j] == k, j, idx)
        return leaf_out[idx]

    leaf_out[LEAF_BLOCKS] = jnp.zeros((BLOCK, BLOCK), BF16)
    r2[...] = jnp.zeros_like(r2)
    r8[...] = jnp.zeros_like(r8)
    loaded(2)
    for i in range(3):
        rows = pl.ds(i * 256, 256)
        depth = (i + 1) * 256
        forward[rows, :] = dot(v_leaf[rows, :depth], v_rhs[:depth, :]).astype(BF16)
    loaded(1)
    for j in range(LEAF_BLOCKS):
        leaf_out[j] = (-dot(v_edge[pl.ds(j * BLOCK, BLOCK), :], forward[...])).astype(BF16)

    pl.semaphore_wait(barrier, len(chips) + 1 + len(members))

    c1 = []
    for i, d in enumerate(members):
        s1[i] = leaf_block(d)
        c1.append(send(s1.at[i], r1.at[i], send_sems.at[0], m1.at[i], (g, d)))
    loaded(2)
    sent.append((s1, send_sems.at[0]))
    total = leaf_block(m).astype(F32)
    for i, c in enumerate(c1):
        c.wait_recv()
        total = total + r1[i].astype(F32)
    s2[...] = total.astype(BF16)
    c2 = []
    for i, d in enumerate(members):
        c = copy_to(s2, r2.at[m], t2.at[i], m2.at[i], (g, d))
        pl.when(d > m)(c.start)
        partial_sends.append((d > m, c))
        c2.append(c)
    r2[m] = s2[...]
    for i, c in enumerate(c2):
        pl.when(sources[i] < m)(c.wait_recv)
    mf = dot(v_mid[...], r2[...].reshape(PIVOTS, BLOCK)).astype(BF16)
    mid_forward[...] = mf

    def border_term(d, b):
        rows = pl.ds(pl.multiple_of(d * 256 + b * BLOCK, BLOCK), BLOCK)
        return leaf_block(PIVOT_BLOCKS + 2 * d + b).astype(F32) - dot(v_border[rows, :], mid_forward[...])

    def half(a, k, h):
        return border_term(lax.rem(mx + a, SIDE) * SIDE + k if h == 0 else k * SIDE + lax.rem(my + a, SIDE), h)

    def along(a, h):
        return (g, member_at(a, 0) if h == 0 else member_at(0, a))

    c3 = []
    for a in NEAR:
        for h in range(2):
            for k in range(SIDE):
                s3[h, a - 1, k] = half(a, k, h).astype(BF16)
            c3.append(send(s3.at[h, a - 1], r3.at[h, a - 1], t3.at[h, a - 1], m3.at[h, a - 1], along(a, h)))
    for h in range(2):
        for k in range(SIDE):
            line[h, k] = half(0, k, h)
    loaded(1)
    for k in range(4):
        for q in range(2):
            t_root[pl.ds(k * BLOCK, BLOCK), pl.ds(q * BLOCK, BLOCK)] = v_root[
                pl.ds(q * BLOCK, BLOCK), pl.ds(k * BLOCK, BLOCK)
            ].T
    for c in c3:
        c.wait_recv()
    sent_copies.extend(c3)
    c3 = []
    here = (my, mx)
    for h in range(2):
        for a in NEAR:
            k = lax.rem(here[h] + a, SIDE)
            total = line[h, k]
            for q in range(3):
                total = total + r3[h, q, k].astype(F32)
            u3[h, a - 1] = total.astype(BF16)
            c3.append(
                send(u3.at[h, a - 1], w3.at[h, a - 1], t3b.at[h, a - 1], m3b.at[h, a - 1], along(a, 1 - h))
            )
    for h in range(2):
        total = line[h, here[h]]
        for q in range(3):
            total = total + r3[h, q, here[h]].astype(F32)
        update[h] = total
    for c in c3:
        c.wait_recv()
    sent_copies.extend(c3)
    for h in range(2):
        total = update[h]
        for q in range(3):
            total = total + w3[h, q].astype(F32)
        update[h] = total
    update[2] = jnp.zeros((BLOCK, BLOCK), F32)

    picks = [root_map[0, 0, i] for i in range(2)]
    for q in range(4):
        idx = jnp.where(picks[0] == q, 0, jnp.where(picks[1] == q, 1, 2))
        s4[pl.ds(q * 4, 4)] = update[idx].astype(BF16).reshape(4, CORES, PIECE, BLOCK)

    def pair_sum(s, pair, u, k):
        c = send(s.at[:, 1 - gc], pair, pair_sems.at[0, k], pair_sems.at[1, k], (other, m))
        c.wait_recv()
        sent_copies.append(c)
        u[...] = (s[:, gc].astype(F32) + pair[...].astype(F32)).astype(BF16)

    def start_sum(u, r, k):
        for i, z in enumerate(chips):
            send(u.at[z], r.at[i], g_sems.at[0, k], g_sems.at[1, k], (z * CORES + gc, m))

    def finish_sum(u, r, k):
        drain(r, g_sems.at[1, k])
        total = u[gz].astype(F32)
        for i in range(len(chips)):
            total = total + r[i].astype(F32)
        sent.append((r, g_sems.at[0, k]))
        return total.astype(BF16)

    def start_gather(r, k):
        for z in chips:
            send(r.at[gz, gc], r.at[gz, gc], g_sems.at[0, k], g_sems.at[1, k], (z * CORES + gc, m))

    def finish_gather(r, k):
        drain(r4, g_sems.at[1, k])
        sent.append((r4, g_sems.at[0, k]))
        c = send(r.at[:, gc], r.at[:, gc], pair_sems.at[0, k], pair_sems.at[1, k], (other, m))
        c.wait_recv()
        sent_copies.append(c)

    pair_sum(s4, p4, u4, 0)
    start_sum(u4, r4, 0)
    for k in range(PIVOT_BLOCKS):
        t_mid[pl.ds(k * BLOCK, BLOCK), :] = v_mid[:, pl.ds(k * BLOCK, BLOCK)].T
    b_root[gz, gc] = finish_sum(u4, r4, 0)
    start_gather(b_root, 1)
    for k in range(BORDER // BLOCK):
        t_border[:, pl.ds(k * BLOCK, BLOCK)] = v_border[pl.ds(k * BLOCK, BLOCK), :].T
    finish_gather(b_root, 1)

    s5[...] = dot(v_root[...], b_root[...].reshape(SHARE, BLOCK)).astype(BF16)
    c5 = []
    for i, d in enumerate(members):
        rows = pl.ds(pl.multiple_of(d * PIECE, PIECE), PIECE)
        c5.append(send(s5.at[rows], r5.at[i], send_sems.at[5], m5, (g, d)))
    sent.append((r5, send_sems.at[5]))
    drain(r5, m5)
    rows = pl.ds(pl.multiple_of(m * PIECE, PIECE), PIECE)
    acc = s5[rows, :].astype(F32)
    for i in range(len(members)):
        acc = acc + r5[i].astype(F32)
    s5b[...] = acc.astype(BF16)
    for i, d in enumerate(members):
        send(s5b, y_root.at[rows], send_sems.at[6], m5b, (g, d))
    y_root[rows, :] = s5b[...]
    sent.append((r5, send_sems.at[6]))
    drain(r5, m5b)

    s6[...] = dot(t_root[...], y_root[...]).astype(BF16).reshape(CHIPS, CORES, PIECE, BLOCK)
    pair_sum(s6, p6, u6, 2)
    start_sum(u6, r6, 2)
    for k in range(LEAF // BLOCK):
        for q in range(EDGE // BLOCK):
            t_edge[pl.ds(k * BLOCK, BLOCK), pl.ds(q * BLOCK, BLOCK)] = v_edge[
                pl.ds(q * BLOCK, BLOCK), pl.ds(k * BLOCK, BLOCK)
            ].T
    x_piece = finish_sum(u6, r6, 2)
    root_o[0] = x_piece
    x_root[gz, gc] = x_piece
    start_gather(x_root, 3)
    for k in range(LEAF // BLOCK):
        for q in range(k, LEAF // BLOCK):
            t_leaf[pl.ds(k * BLOCK, BLOCK), pl.ds(q * BLOCK, BLOCK)] = v_leaf[
                pl.ds(q * BLOCK, BLOCK), pl.ds(k * BLOCK, BLOCK)
            ].T
        for q in range(k - k % 2, k):
            t_leaf[pl.ds(k * BLOCK, BLOCK), pl.ds(q * BLOCK, BLOCK)] = v_leaf[
                pl.ds(q * BLOCK, BLOCK), pl.ds(k * BLOCK, BLOCK)
            ].T
    finish_gather(x_root, 3)
    x_blocks[...] = x_root[...].reshape(4, BLOCK, BLOCK)

    for h in range(2):
        front[PIVOT_BLOCKS + 2 * m + h] = x_blocks[picks[h]]

    def forward_block(a, b, h, to):
        k = PIVOT_BLOCKS + 2 * member_at((SIDE - a) % SIDE, (SIDE - b) % SIDE) + h
        a2, b2 = a + to[0], b + to[1]
        c = send(front.at[k], front.at[k], t7.at[h, a2, b2], m7.at[h, a2, b2], (g, member_at(*to)))
        sent_copies.append(c)
        return c

    c7 = {}
    for a in NEAR:
        c7[0, a, 0] = forward_block(0, 0, 0, (a, 0))
        c7[1, 0, a] = forward_block(0, 0, 1, (0, a))
    for a in NEAR:
        c7[0, 0, a] = forward_block(0, 0, 0, (0, a))
        c7[1, a, 0] = forward_block(0, 0, 1, (a, 0))
    for a in (1, 3, 2):
        c7.pop((0, a, 0)).wait_recv()
        for b in NEAR:
            c7[0, a, b] = forward_block(a, 0, 0, (0, b))
        c7.pop((1, 0, a)).wait_recv()
        for b in NEAR:
            c7[1, b, a] = forward_block(0, a, 1, (b, 0))
    for c in c7.values():
        c.wait_recv()
    back = dot(t_border[...], front[PIVOT_BLOCKS:].reshape(BORDER, BLOCK))
    mid_back[...] = (mid_forward[...].astype(F32) - back).astype(BF16)

    def mid_term(d):
        rows = pl.ds(pl.multiple_of(d * BLOCK, BLOCK), BLOCK)
        return dot(t_mid[rows, :], mid_back[...])

    c8 = []
    for i, d in enumerate(members):
        c = copy_to(s8.at[i], r8.at[i], t8.at[i], m8.at[i], (g, d))

        @pl.when(d < m)
        def _(i=i, d=d, c=c):
            s8[i] = mid_term(d).astype(BF16)
            c.start()

        partial_sends.append((d < m, c))
        c8.append(c)
    total = mid_term(m)
    for i, c in enumerate(c8):
        pl.when(sources[i] > m)(c.wait_recv)
    for i in range(len(c8)):
        total = total + r8[i].astype(F32)
    front[m] = total.astype(BF16)
    mid_o[0] = total.astype(BF16)
    c8b = []
    for i, d in enumerate(members):
        c8b.append(send(front.at[m], front.at[m], send_sems.at[11], m8b.at[i], (g, d)))
    sent.append((s1, send_sems.at[11]))
    for c in c8b:
        c.wait_recv()

    lb = forward[...].astype(F32)
    for j in range(LEAF_BLOCKS):
        lb = lb - dot(t_edge[:, pl.ds(j * BLOCK, BLOCK)], front[targets[j]])
    lb = lb.astype(BF16)
    for i in range(3):
        leaf_o[0, 0, pl.ds(i * 256, 256), :] = dot(
            t_leaf[pl.ds(i * 256, 256), i * 256 :], lb[i * 256 :]
        ).astype(BF16)

    finish()


def write_out(*refs):
    n = len(refs) // 2
    copies = [pltpu.make_async_copy(refs[i], refs[n + i], refs[-1].at[i]) for i in range(n)]
    for c in copies:
        c.start()
    for c in copies:
        c.wait()


def on_device(rhs, leaf_inverse, leaf_edge, leaf_map, *rest):
    args = (rhs, leaf_inverse, leaf_edge, jnp.swapaxes(leaf_map, 1, 2), *rest)
    n_m, n_z = MEMBERS - 1, CHIPS - 1
    piece = (PIECE, BLOCK)
    dma = pltpu.SemaphoreType.DMA
    block = (BLOCK, BLOCK)
    v = lambda *shape: pltpu.VMEM(shape, BF16)
    scratch = [
        v(LEAF, BLOCK),
        v(LEAF, LEAF),
        v(EDGE, LEAF),
        v(BLOCK, PIVOTS),
        v(BORDER, BLOCK),
        v(ROOT_ROWS, SHARE),
        v(LEAF, LEAF),
        v(LEAF, EDGE),
        v(PIVOTS, BLOCK),
        v(BLOCK, BORDER),
        v(SHARE, ROOT_ROWS),
        v(LEAF, BLOCK),
        v(LEAF_BLOCKS + 1, *block),
        v(n_m, *block),
        v(n_m, *block),
        v(*block),
        v(MEMBERS, *block),
        v(*block),
        v(2, 3, SIDE, *block),
        v(2, 3, SIDE, *block),
        pltpu.VMEM((2, SIDE, *block), F32),
        v(2, 3, *block),
        v(2, 3, *block),
        pltpu.VMEM((3, *block), F32),
        v(CHIPS, CORES, *piece),
        v(CHIPS, *piece),
        v(CHIPS, *piece),
        v(n_z, *piece),
        v(CHIPS, CORES, *piece),
        v(ROOT_ROWS, BLOCK),
        v(n_m, *piece),
        v(*piece),
        v(ROOT_ROWS, BLOCK),
        v(CHIPS, CORES, *piece),
        v(CHIPS, *piece),
        v(CHIPS, *piece),
        v(n_z, *piece),
        v(CHIPS, CORES, *piece),
        v(4, *block),
        v(FRONT_BLOCKS, *block),
        v(*block),
        v(n_m, *block),
        v(n_m, *block),
        dma((6,)),
        dma((12,)),
        dma((n_m,)),
        dma((n_m,)),
        dma((n_m,)),
        dma((2, 3)),
        dma((2, 3)),
        dma((2, 3)),
        dma((2, 3)),
        dma,
        dma,
        dma((2, SIDE, SIDE)),
        dma((2, SIDE, SIDE)),
        dma((n_m,)),
        dma((n_m,)),
        dma((n_m,)),
        dma((2, 4)),
        dma((2, 4)),
    ]
    anywhere = pl.BlockSpec(memory_space=pltpu.HBM)
    scalars = pl.BlockSpec(memory_space=pltpu.SMEM)
    vmem = pl.BlockSpec(memory_space=pltpu.VMEM)
    shapes = (
            jax.ShapeDtypeStruct((1, 1, LEAF, BLOCK), BF16),
            jax.ShapeDtypeStruct((1, BLOCK, BLOCK), BF16),
            jax.ShapeDtypeStruct((1, PIECE, BLOCK), BF16),
    )
    values = pl.pallas_call(
        whole_kernel,
        out_shape=shapes,
        in_specs=[anywhere, anywhere, anywhere, scalars, anywhere, anywhere, scalars, anywhere],
        out_specs=(vmem, vmem, vmem),
        scratch_shapes=scratch,
        name="solve",
        compiler_params=pltpu.CompilerParams(
            collective_id=0, has_side_effects=True, vmem_limit_bytes=63_000_000
        ),
    )(*args)
    return pl.pallas_call(
        write_out,
        out_shape=shapes,
        in_specs=[anywhere] * 3,
        out_specs=(anywhere,) * 3,
        scratch_shapes=[dma((3,))],
        name="write",
    )(*values)


def solution(mesh):
    in_specs = (
        P("group", "member", None, None),
        P("group", "member", None, None),
        P("group", "member", None, None),
        P("group", None, None),
        P("group", "member", None),
        P("group", None, "member"),
        P("group", "member", None),
        P("group", "member"),
    )
    out_specs = (
        P("group", "member", None, None),
        P("group", "member", None),
        P("member", "group", None),
    )
    return jax.shard_map(
        on_device, mesh=mesh, in_specs=in_specs, out_specs=out_specs, check_vma=False
    )
```

```python
import functools

import jax
import jax.numpy as jnp
from jax import lax
from jax.experimental import pallas as pl
from jax.experimental.pallas import tpu as pltpu
from jax.sharding import PartitionSpec as P

BLOCK = 128
SIDE = 4
MEMBERS = 16
CORES = 2
CHIPS = 16
LEAF = 768
EDGE = 512
LEAF_BLOCKS = EDGE // BLOCK
PIVOTS = 2048
PIVOT_BLOCKS = PIVOTS // BLOCK
BORDER = 4096
FRONT_BLOCKS = (PIVOTS + BORDER) // BLOCK
SHARE = 512
ROOT_ROWS = 256
PIECE = 16
MESH = pl.DeviceIdType.MESH
F32 = jnp.float32
BF16 = jnp.bfloat16

MEMBER_OFFSETS = [
    (2, 2),
    (2, 1),
    (1, 2),
    (2, 3),
    (3, 2),
    (1, 1),
    (3, 3),
    (1, 3),
    (3, 1),
    (2, 0),
    (0, 2),
    (1, 0),
    (3, 0),
    (0, 1),
    (0, 3),
]
CHIP_OFFSETS = sorted(range(1, CHIPS), key=lambda a: -min(a, CHIPS - a))
HALF_RING = CHIPS // 2
HALF_OFFSETS = (4, 3, 13, 2, 14, 1, 15)
SLICE = 32
NEAR = (2, 1, 3)


def dot(a, b):
    return jnp.dot(a, b, preferred_element_type=F32)


def whole_kernel(
    rhs,
    leaf_inverse,
    leaf_edge,
    leaf_map,
    mid_inverse,
    mid_border,
    root_map,
    root_inverse,
    leaf_o,
    mid_o,
    root_o,
    v_rhs,
    v_leaf,
    v_edge,
    v_mid,
    v_border,
    v_root,
    t_leaf,
    t_edge,
    t_mid,
    t_border,
    t_root,
    forward,
    leaf_out,
    s1,
    r1,
    s2,
    r2,
    mid_forward,
    s3,
    r3,
    line,
    u3,
    w3,
    update,
    s4,
    p4,
    u4,
    r4,
    b_root,
    s5,
    r5,
    s5b,
    y_root,
    s6,
    p6,
    u6,
    r6,
    x_root,
    x_blocks,
    front,
    mid_back,
    s8,
    r8,
    load_sems,
    send_sems,
    m1,
    t2,
    m2,
    t3,
    m3,
    t3b,
    m3b,
    m5,
    m5b,
    t7,
    m7,
    t8,
    m8,
    m8b,
    g_sems,
    pair_sems,
):
    g = lax.axis_index("group")
    m = lax.axis_index("member")
    mx, my = m // SIDE, lax.rem(m, SIDE)
    gz, gc = g // CORES, lax.rem(g, CORES)
    other = gz * CORES + 1 - gc

    def member_at(a, b):
        return lax.rem(mx + a, SIDE) * SIDE + lax.rem(my + b, SIDE)

    members, sources = [], []
    for a, b in MEMBER_OFFSETS:
        up, down = member_at(a, b), member_at((SIDE - a) % SIDE, (SIDE - b) % SIDE)
        members.append(jnp.where(gc == 0, up, down))
        sources.append(jnp.where(gc == 0, down, up))
    chips = [lax.rem(gz + a, CHIPS) for a in CHIP_OFFSETS]
    half_ring = [
        lax.rem(gz + jnp.where(gc == 0, a, CHIPS - a), CHIPS) for a in HALF_OFFSETS
    ]
    gp = lax.rem(gz, HALF_RING)

    barrier = pltpu.get_barrier_semaphore()
    for z in chips:
        pl.semaphore_signal(barrier, inc=1, device_id=(z * CORES + gc, m), device_id_type=MESH)
    pl.semaphore_signal(barrier, inc=1, device_id=(other, m), device_id_type=MESH)
    for d in members:
        pl.semaphore_signal(barrier, inc=1, device_id=(g, d), device_id_type=MESH)

    loads = []
    for i, (src, dst) in enumerate(
        [
            (rhs.at[0, 0], v_rhs),
            (leaf_inverse.at[0, 0], v_leaf),
            (leaf_edge.at[0, 0], v_edge),
            (mid_inverse.at[0], v_mid),
            (mid_border.at[0], v_border),
            (root_inverse, v_root),
        ]
    ):
        c = pltpu.make_async_copy(src, dst, load_sems.at[i])
        c.start()
        loads.append(c)

    def copy_to(src, dst, ssem, rsem, device):
        return pltpu.make_async_remote_copy(
            src_ref=src,
            dst_ref=dst,
            send_sem=ssem,
            recv_sem=rsem,
            device_id=device,
            device_id_type=MESH,
        )

    def send(*args):
        c = copy_to(*args)
        c.start()
        return c

    def drain(ref, sem):
        pltpu.make_async_copy(ref, ref, sem).wait()

    sent = []
    partial_sends = []
    sent_copies = []
    pending = list(loads)

    def loaded(n):
        for _ in range(n):
            pending.pop(0).wait()

    def finish():
        loaded(len(pending))
        for ref, i in sent:
            drain(ref, i)
        for when, c in partial_sends:
            pl.when(when)(c.wait_send)
        for c in sent_copies:
            c.wait_send()

    targets = [leaf_map[0, j, m] for j in range(LEAF_BLOCKS)]

    def leaf_block(k):
        idx = jnp.int32(LEAF_BLOCKS)
        for j in range(LEAF_BLOCKS):
            idx = jnp.where(targets[j] == k, j, idx)
        return leaf_out[idx]

    leaf_out[LEAF_BLOCKS] = jnp.zeros((BLOCK, BLOCK), BF16)
    r2[...] = jnp.zeros_like(r2)
    r8[...] = jnp.zeros_like(r8)
    loaded(2)
    for i in range(3):
        rows = pl.ds(i * 256, 256)
        depth = (i + 1) * 256
        forward[rows, :] = dot(v_leaf[rows, :depth], v_rhs[:depth, :]).astype(BF16)
    loaded(1)
    for j in range(LEAF_BLOCKS):
        leaf_out[j] = (-dot(v_edge[pl.ds(j * BLOCK, BLOCK), :], forward[...])).astype(BF16)

    pl.semaphore_wait(barrier, len(chips) + 1 + len(members))

    c1 = []
    for i, d in enumerate(members):
        s1[i] = leaf_block(d)
        c1.append(send(s1.at[i], r1.at[i], send_sems.at[0], m1.at[i], (g, d)))
    loaded(2)
    sent.append((s1, send_sems.at[0]))
    total = leaf_block(m).astype(F32)
    for i, c in enumerate(c1):
        c.wait_recv()
        total = total + r1[i].astype(F32)
    s2[...] = total.astype(BF16)
    c2 = []
    for i, d in enumerate(members):
        c = copy_to(s2, r2.at[m], t2.at[i], m2.at[i], (g, d))
        pl.when(d > m)(c.start)
        partial_sends.append((d > m, c))
        c2.append(c)
    r2[m] = s2[...]
    for i, c in enumerate(c2):
        pl.when(sources[i] < m)(c.wait_recv)
    mf = dot(v_mid[...], r2[...].reshape(PIVOTS, BLOCK)).astype(BF16)
    mid_forward[...] = mf

    def terms(a, h):
        at = lax.rem((mx, my)[h] + a, SIDE)
        rows = v_border[at, :, h] if h == 0 else v_border[:, at, h]
        product = dot(rows.reshape(SIDE * BLOCK, BLOCK), mid_forward[...])
        out = []
        for k in range(SIDE):
            d = at * SIDE + k if h == 0 else k * SIDE + at
            out.append(
                leaf_block(PIVOT_BLOCKS + 2 * d + h).astype(F32) - product[k * BLOCK : (k + 1) * BLOCK]
            )
        return out

    def along(a, h):
        return (g, member_at(a, 0) if h == 0 else member_at(0, a))

    c3 = []
    for a in NEAR:
        for h in range(2):
            for k, term in enumerate(terms(a, h)):
                s3[h, a - 1, k] = term.astype(BF16)
            c3.append(send(s3.at[h, a - 1], r3.at[h, a - 1], t3.at[h, a - 1], m3.at[h, a - 1], along(a, h)))
    for h in range(2):
        for k, term in enumerate(terms(0, h)):
            line[h, k] = term
    loaded(1)
    for k in range(4):
        for q in range(2):
            t_root[pl.ds(k * BLOCK, BLOCK), pl.ds(q * BLOCK, BLOCK)] = v_root[
                pl.ds(q * BLOCK, BLOCK), pl.ds(k * BLOCK, BLOCK)
            ].T
    for c in c3:
        c.wait_recv()
    sent_copies.extend(c3)
    c3 = []
    here = (my, mx)
    for h in range(2):
        for a in NEAR:
            k = lax.rem(here[h] + a, SIDE)
            total = line[h, k]
            for q in range(3):
                total = total + r3[h, q, k].astype(F32)
            u3[h, a - 1] = total.astype(BF16)
            c3.append(
                send(u3.at[h, a - 1], w3.at[h, a - 1], t3b.at[h, a - 1], m3b.at[h, a - 1], along(a, 1 - h))
            )
    for h in range(2):
        total = line[h, here[h]]
        for q in range(3):
            total = total + r3[h, q, here[h]].astype(F32)
        update[h] = total
    for c in c3:
        c.wait_recv()
    sent_copies.extend(c3)
    for h in range(2):
        total = update[h]
        for q in range(3):
            total = total + w3[h, q].astype(F32)
        update[h] = total
    update[2] = jnp.zeros((BLOCK, BLOCK), F32)

    picks = [root_map[0, 0, i] for i in range(2)]
    for q in range(4):
        idx = jnp.where(picks[0] == q, 0, jnp.where(picks[1] == q, 1, 2))
        s4[pl.ds(q * 2, 2)] = update[idx].astype(BF16).reshape(2, CORES, SLICE, BLOCK)

    def pair_sum(s, pair, u, k):
        c = send(s.at[:, 1 - gc], pair, pair_sems.at[0, k], pair_sems.at[1, k], (other, m))
        c.wait_recv()
        sent_copies.append(c)
        u[...] = (s[:, gc].astype(F32) + pair[...].astype(F32)).astype(BF16)

    def start_sum(u, r, k):
        for i, z in enumerate(chips):
            send(u.at[lax.rem(z, HALF_RING)], r.at[i], g_sems.at[0, k], g_sems.at[1, k], (z * CORES + gc, m))

    def finish_sum(u, r, k):
        drain(r, g_sems.at[1, k])
        total = u[gp].astype(F32)
        for i in range(len(chips)):
            total = total + r[i].astype(F32)
        sent.append((r, g_sems.at[0, k]))
        return total.astype(BF16)

    def start_gather(r, k):
        for z in half_ring:
            send(r.at[gp, gc], r.at[gp, gc], g_sems.at[0, k], g_sems.at[1, k], (z * CORES + gc, m))

    def finish_gather(r, k):
        seven = u4.at[: len(half_ring)]
        drain(seven, g_sems.at[1, k])
        sent.append((seven, g_sems.at[0, k]))
        c = send(r.at[:, gc], r.at[:, gc], pair_sems.at[0, k], pair_sems.at[1, k], (other, m))
        c.wait_recv()
        sent_copies.append(c)

    pair_sum(s4, p4, u4, 0)
    start_sum(u4, r4, 0)
    for k in range(PIVOT_BLOCKS):
        t_mid[pl.ds(k * BLOCK, BLOCK), :] = v_mid[:, pl.ds(k * BLOCK, BLOCK)].T
    b_root[gp, gc] = finish_sum(u4, r4, 0)
    start_gather(b_root, 1)
    for k in range(BORDER // BLOCK):
        t_border[:, pl.ds(k * BLOCK, BLOCK)] = v_border[k // 8, k // 2 % 4, k % 2].T
    finish_gather(b_root, 1)

    s5[...] = dot(v_root[...], b_root[...].reshape(SHARE, BLOCK)).astype(BF16)
    c5 = []
    for i, d in enumerate(members):
        rows = pl.ds(pl.multiple_of(d * PIECE, PIECE), PIECE)
        c5.append(send(s5.at[rows], r5.at[i], send_sems.at[5], m5, (g, d)))
    sent.append((r5, send_sems.at[5]))
    drain(r5, m5)
    rows = pl.ds(pl.multiple_of(m * PIECE, PIECE), PIECE)
    acc = s5[rows, :].astype(F32)
    for i in range(len(members)):
        acc = acc + r5[i].astype(F32)
    s5b[...] = acc.astype(BF16)
    for i, d in enumerate(members):
        send(s5b, y_root.at[rows], send_sems.at[6], m5b, (g, d))
    y_root[rows, :] = s5b[...]
    sent.append((r5, send_sems.at[6]))
    drain(r5, m5b)

    s6[...] = dot(t_root[...], y_root[...]).astype(BF16).reshape(HALF_RING, CORES, SLICE, BLOCK)
    pair_sum(s6, p6, u6, 2)
    start_sum(u6, r6, 2)
    for k in range(LEAF // BLOCK):
        for q in range(EDGE // BLOCK):
            t_edge[pl.ds(k * BLOCK, BLOCK), pl.ds(q * BLOCK, BLOCK)] = v_edge[
                pl.ds(q * BLOCK, BLOCK), pl.ds(k * BLOCK, BLOCK)
            ].T
    x_root[gp, gc] = finish_sum(u6, r6, 2)
    start_gather(x_root, 3)
    for k in range(LEAF // BLOCK):
        for q in range(k, LEAF // BLOCK):
            t_leaf[pl.ds(k * BLOCK, BLOCK), pl.ds(q * BLOCK, BLOCK)] = v_leaf[
                pl.ds(q * BLOCK, BLOCK), pl.ds(k * BLOCK, BLOCK)
            ].T
        for q in range(k - k % 2, k):
            t_leaf[pl.ds(k * BLOCK, BLOCK), pl.ds(q * BLOCK, BLOCK)] = v_leaf[
                pl.ds(q * BLOCK, BLOCK), pl.ds(k * BLOCK, BLOCK)
            ].T
    finish_gather(x_root, 3)
    x_blocks[...] = x_root[...].reshape(4, BLOCK, BLOCK)
    out_rows = pl.ds(pl.multiple_of(lax.rem(g, 2) * PIECE, PIECE), PIECE)
    root_o[0] = x_root[g // 4, lax.rem(g // 2, 2), out_rows]

    for h in range(2):
        front[PIVOT_BLOCKS + 2 * m + h] = x_blocks[picks[h]]

    def forward_block(a, b, h, to):
        k = PIVOT_BLOCKS + 2 * member_at((SIDE - a) % SIDE, (SIDE - b) % SIDE) + h
        a2, b2 = a + to[0], b + to[1]
        c = send(front.at[k], front.at[k], t7.at[h, a2, b2], m7.at[h, a2, b2], (g, member_at(*to)))
        sent_copies.append(c)
        return c

    c7 = {}
    for a in NEAR:
        c7[0, a, 0] = forward_block(0, 0, 0, (a, 0))
        c7[1, 0, a] = forward_block(0, 0, 1, (0, a))
    for a in NEAR:
        c7[0, 0, a] = forward_block(0, 0, 0, (0, a))
        c7[1, a, 0] = forward_block(0, 0, 1, (a, 0))
    for a in (1, 3, 2):
        c7.pop((0, a, 0)).wait_recv()
        for b in NEAR:
            c7[0, a, b] = forward_block(a, 0, 0, (0, b))
        c7.pop((1, 0, a)).wait_recv()
        for b in NEAR:
            c7[1, b, a] = forward_block(0, a, 1, (b, 0))
    for c in c7.values():
        c.wait_recv()
    back = dot(t_border[...], front[PIVOT_BLOCKS:].reshape(BORDER, BLOCK))
    mid_back[...] = (mid_forward[...].astype(F32) - back).astype(BF16)

    c8 = []
    for d in range(MEMBERS):
        c8.append(copy_to(s8.at[d], r8.at[m], t8.at[d], m8.at[m], (g, d)))
    for q in range(SIDE):

        @pl.when(q <= mx)
        def _(q=q):
            product = dot(t_mid[pl.ds(q * SHARE, SHARE), :], mid_back[...])
            s8[pl.ds(q * SIDE, SIDE)] = product.astype(BF16).reshape(SIDE, BLOCK, BLOCK)
            for d in range(q * SIDE, (q + 1) * SIDE):
                pl.when(d < m)(c8[d].start)

    for d in range(MEMBERS):
        partial_sends.append((d < m, c8[d]))
    total = s8[m].astype(F32)
    for d in range(MEMBERS):
        c = copy_to(s8.at[d], r8.at[d], t8.at[d], m8.at[d], (g, d))
        pl.when(d > m)(c.wait_recv)
        total = total + r8[d].astype(F32)
    front[m] = total.astype(BF16)
    mid_o[0] = total.astype(BF16)
    c8b = []
    for i, d in enumerate(members):
        c8b.append(send(front.at[m], front.at[m], send_sems.at[11], m8b.at[i], (g, d)))
    sent.append((s1, send_sems.at[11]))
    for c in c8b:
        c.wait_recv()

    lb = forward[...].astype(F32)
    for j in range(LEAF_BLOCKS):
        lb = lb - dot(t_edge[:, pl.ds(j * BLOCK, BLOCK)], front[targets[j]])
    lb = lb.astype(BF16)
    for i in range(3):
        leaf_o[0, 0, pl.ds(i * 256, 256), :] = dot(
            t_leaf[pl.ds(i * 256, 256), i * 256 :], lb[i * 256 :]
        ).astype(BF16)

    finish()


def write_out(*refs):
    for src, dst in zip(refs[:3], refs[3:]):
        dst[...] = src[...]


def on_device(rhs, leaf_inverse, leaf_edge, leaf_map, mid_inverse, mid_border, *rest):
    blocks = mid_border.reshape(1, SIDE, SIDE, 2, BLOCK, BLOCK)
    args = (rhs, leaf_inverse, leaf_edge, jnp.swapaxes(leaf_map, 1, 2), mid_inverse, blocks, *rest)
    n_m, n_z = MEMBERS - 1, CHIPS - 1
    piece = (PIECE, BLOCK)
    part = (SLICE, BLOCK)
    dma = pltpu.SemaphoreType.DMA
    block = (BLOCK, BLOCK)
    v = lambda *shape: pltpu.VMEM(shape, BF16)
    scratch = [
        v(LEAF, BLOCK),
        v(LEAF, LEAF),
        v(EDGE, LEAF),
        v(BLOCK, PIVOTS),
        v(SIDE, SIDE, 2, *block),
        v(ROOT_ROWS, SHARE),
        v(LEAF, LEAF),
        v(LEAF, EDGE),
        v(PIVOTS, BLOCK),
        v(BLOCK, BORDER),
        v(SHARE, ROOT_ROWS),
        v(LEAF, BLOCK),
        v(LEAF_BLOCKS + 1, *block),
        v(n_m, *block),
        v(n_m, *block),
        v(*block),
        v(MEMBERS, *block),
        v(*block),
        v(2, 3, SIDE, *block),
        v(2, 3, SIDE, *block),
        pltpu.VMEM((2, SIDE, *block), F32),
        v(2, 3, *block),
        v(2, 3, *block),
        pltpu.VMEM((3, *block), F32),
        v(HALF_RING, CORES, *part),
        v(HALF_RING, *part),
        v(HALF_RING, *part),
        v(n_z, *part),
        v(HALF_RING, CORES, *part),
        v(ROOT_ROWS, BLOCK),
        v(n_m, *piece),
        v(*piece),
        v(ROOT_ROWS, BLOCK),
        v(HALF_RING, CORES, *part),
        v(HALF_RING, *part),
        v(HALF_RING, *part),
        v(n_z, *part),
        v(HALF_RING, CORES, *part),
        v(4, *block),
        v(FRONT_BLOCKS, *block),
        v(*block),
        v(MEMBERS, *block),
        v(MEMBERS, *block),
        dma((6,)),
        dma((12,)),
        dma((n_m,)),
        dma((n_m,)),
        dma((n_m,)),
        dma((2, 3)),
        dma((2, 3)),
        dma((2, 3)),
        dma((2, 3)),
        dma,
        dma,
        dma((2, SIDE, SIDE)),
        dma((2, SIDE, SIDE)),
        dma((MEMBERS,)),
        dma((MEMBERS,)),
        dma((n_m,)),
        dma((2, 4)),
        dma((2, 4)),
    ]
    anywhere = pl.BlockSpec(memory_space=pltpu.HBM)
    scalars = pl.BlockSpec(memory_space=pltpu.SMEM)
    vmem = pl.BlockSpec(memory_space=pltpu.VMEM)
    shapes = (
            jax.ShapeDtypeStruct((1, 1, LEAF, BLOCK), BF16),
            jax.ShapeDtypeStruct((1, BLOCK, BLOCK), BF16),
            jax.ShapeDtypeStruct((1, PIECE, BLOCK), BF16),
    )
    values = pl.pallas_call(
        whole_kernel,
        out_shape=shapes,
        in_specs=[anywhere, anywhere, anywhere, scalars, anywhere, anywhere, scalars, anywhere],
        out_specs=(vmem, vmem, vmem),
        scratch_shapes=scratch,
        name="solve",
        compiler_params=pltpu.CompilerParams(
            collective_id=0, has_side_effects=True, vmem_limit_bytes=63_000_000
        ),
    )(*args)
    return pl.pallas_call(
        write_out,
        out_shape=shapes,
        in_specs=[vmem] * 3,
        out_specs=(vmem,) * 3,
        name="write",
    )(*values)


def solution(mesh):
    in_specs = (
        P("group", "member", None, None),
        P("group", "member", None, None),
        P("group", "member", None, None),
        P("group", None, None),
        P("group", "member", None),
        P("group", None, "member"),
        P("group", "member", None),
        P("group", "member"),
    )
    out_specs = (
        P("group", "member", None, None),
        P("group", "member", None),
        P("member", "group", None),
    )
    return jax.shard_map(
        on_device, mesh=mesh, in_specs=in_specs, out_specs=out_specs, check_vma=False
    )
```

```python
import functools

import jax
import jax.numpy as jnp
from jax import lax
from jax.experimental import pallas as pl
from jax.experimental.pallas import tpu as pltpu
from jax.sharding import PartitionSpec as P

BLOCK = 128
SIDE = 4
MEMBERS = 16
CORES = 2
CHIPS = 16
LEAF = 768
EDGE = 512
LEAF_BLOCKS = EDGE // BLOCK
PIVOTS = 2048
PIVOT_BLOCKS = PIVOTS // BLOCK
BORDER = 4096
FRONT_BLOCKS = (PIVOTS + BORDER) // BLOCK
SHARE = 512
ROOT_ROWS = 256
PIECE = 16
MESH = pl.DeviceIdType.MESH
F32 = jnp.float32
BF16 = jnp.bfloat16

MEMBER_OFFSETS = [
    (2, 2),
    (2, 1),
    (1, 2),
    (2, 3),
    (3, 2),
    (1, 1),
    (3, 3),
    (1, 3),
    (3, 1),
    (2, 0),
    (0, 2),
    (1, 0),
    (3, 0),
    (0, 1),
    (0, 3),
]
CHIP_OFFSETS = sorted(range(1, CHIPS), key=lambda a: -min(a, CHIPS - a))
HALF_RING = CHIPS // 2
HALF_OFFSETS = (4, 3, 13, 2, 14, 1, 15)
SLICE = 32
NEAR = (2, 1, 3)


def dot(a, b):
    return jnp.dot(a, b, preferred_element_type=F32)


def whole_kernel(
    rhs,
    leaf_inverse,
    leaf_edge,
    leaf_map,
    mid_inverse,
    mid_border,
    root_map,
    root_inverse,
    leaf_o,
    mid_o,
    root_o,
    v_rhs,
    v_leaf,
    v_edge,
    v_mid,
    v_border,
    v_root,
    v_root2,
    t_leaf,
    t_edge,
    t_mid,
    t_border,
    t_root,
    t_root2,
    forward,
    leaf_out,
    s1,
    r1,
    s2,
    r2,
    mid_forward,
    s3,
    r3,
    line,
    u3,
    w3,
    update,
    s4,
    q4,
    p4,
    u4,
    r4,
    b_root,
    s5,
    r5,
    s5b,
    y_root,
    u6,
    r6,
    x_half,
    x_other,
    x_root,
    x_blocks,
    front,
    mid_back,
    s8,
    r8,
    load_sems,
    send_sems,
    m1,
    t2,
    m2,
    t3,
    m3,
    t3b,
    m3b,
    m5,
    m5b,
    t7,
    m7,
    t8,
    m8,
    m8b,
    g_sems,
    pair_sems,
):
    g = lax.axis_index("group")
    m = lax.axis_index("member")
    mx, my = m // SIDE, lax.rem(m, SIDE)
    gz, gc = g // CORES, lax.rem(g, CORES)
    other = gz * CORES + 1 - gc

    def member_at(a, b):
        return lax.rem(mx + a, SIDE) * SIDE + lax.rem(my + b, SIDE)

    members, sources = [], []
    for a, b in MEMBER_OFFSETS:
        up, down = member_at(a, b), member_at((SIDE - a) % SIDE, (SIDE - b) % SIDE)
        members.append(jnp.where(gc == 0, up, down))
        sources.append(jnp.where(gc == 0, down, up))
    chips = [lax.rem(gz + a, CHIPS) for a in CHIP_OFFSETS]
    half_ring = [
        lax.rem(gz + jnp.where(gc == 0, a, CHIPS - a), CHIPS) for a in HALF_OFFSETS
    ]
    gp = lax.rem(gz, HALF_RING)

    barrier = pltpu.get_barrier_semaphore()
    for z in chips:
        pl.semaphore_signal(barrier, inc=1, device_id=(z * CORES + gc, m), device_id_type=MESH)
    pl.semaphore_signal(barrier, inc=1, device_id=(other, m), device_id_type=MESH)
    for d in members:
        pl.semaphore_signal(barrier, inc=1, device_id=(g, d), device_id_type=MESH)

    loads = []
    for i, (src, dst) in enumerate(
        [
            (rhs.at[0, 0], v_rhs),
            (leaf_inverse.at[0, 0], v_leaf),
            (leaf_edge.at[0, 0], v_edge),
            (root_inverse, v_root),
            (mid_inverse.at[0], v_mid),
            (mid_border.at[0], v_border),
        ]
    ):
        c = pltpu.make_async_copy(src, dst, load_sems.at[i])
        c.start()
        loads.append(c)

    def copy_to(src, dst, ssem, rsem, device):
        return pltpu.make_async_remote_copy(
            src_ref=src,
            dst_ref=dst,
            send_sem=ssem,
            recv_sem=rsem,
            device_id=device,
            device_id_type=MESH,
        )

    def send(*args):
        c = copy_to(*args)
        c.start()
        return c

    def drain(ref, sem):
        pltpu.make_async_copy(ref, ref, sem).wait()

    sent = []
    partial_sends = []
    sent_copies = []
    pending = list(loads)

    def loaded(n):
        for _ in range(n):
            pending.pop(0).wait()

    def finish():
        loaded(len(pending))
        for ref, i in sent:
            drain(ref, i)
        for when, c in partial_sends:
            pl.when(when)(c.wait_send)
        for c in sent_copies:
            c.wait_send()

    targets = [leaf_map[0, j, m] for j in range(LEAF_BLOCKS)]

    def leaf_block(k):
        idx = jnp.int32(LEAF_BLOCKS)
        for j in range(LEAF_BLOCKS):
            idx = jnp.where(targets[j] == k, j, idx)
        return leaf_out[idx]

    leaf_out[LEAF_BLOCKS] = jnp.zeros((BLOCK, BLOCK), BF16)
    r2[...] = jnp.zeros_like(r2)
    r8[...] = jnp.zeros_like(r8)
    loaded(2)
    for i in range(3):
        rows = pl.ds(i * 256, 256)
        depth = (i + 1) * 256
        forward[rows, :] = dot(v_leaf[rows, :depth], v_rhs[:depth, :]).astype(BF16)
    loaded(1)
    for j in range(LEAF_BLOCKS):
        leaf_out[j] = (-dot(v_edge[pl.ds(j * BLOCK, BLOCK), :], forward[...])).astype(BF16)

    pl.semaphore_wait(barrier, len(chips) + 1 + len(members))

    loaded(1)
    c_root = send(v_root, v_root2, pair_sems.at[0, 1], pair_sems.at[1, 1], (other, m))
    sent_copies.append(c_root)
    c1 = []
    for i, d in enumerate(members):
        s1[i] = leaf_block(d)
        c1.append(send(s1.at[i], r1.at[i], send_sems.at[0], m1.at[i], (g, d)))
    loaded(2)
    sent.append((s1, send_sems.at[0]))
    total = leaf_block(m).astype(F32)
    for i, c in enumerate(c1):
        c.wait_recv()
        total = total + r1[i].astype(F32)
    s2[...] = total.astype(BF16)
    c2 = []
    for i, d in enumerate(members):
        c = copy_to(s2, r2.at[m], t2.at[i], m2.at[i], (g, d))
        pl.when(d > m)(c.start)
        partial_sends.append((d > m, c))
        c2.append(c)
    r2[m] = s2[...]
    for i, c in enumerate(c2):
        pl.when(sources[i] < m)(c.wait_recv)
    mf = dot(v_mid[...], r2[...].reshape(PIVOTS, BLOCK)).astype(BF16)
    mid_forward[...] = mf

    def terms(a, h):
        at = lax.rem((mx, my)[h] + a, SIDE)
        rows = v_border[at, :, h] if h == 0 else v_border[:, at, h]
        product = dot(rows.reshape(SIDE * BLOCK, BLOCK), mid_forward[...])
        out = []
        for k in range(SIDE):
            d = at * SIDE + k if h == 0 else k * SIDE + at
            out.append(
                leaf_block(PIVOT_BLOCKS + 2 * d + h).astype(F32) - product[k * BLOCK : (k + 1) * BLOCK]
            )
        return out

    def along(a, h):
        return (g, member_at(a, 0) if h == 0 else member_at(0, a))

    c3 = []
    for a in NEAR:
        for h in range(2):
            for k, term in enumerate(terms(a, h)):
                s3[h, a - 1, k] = term.astype(BF16)
            c3.append(send(s3.at[h, a - 1], r3.at[h, a - 1], t3.at[h, a - 1], m3.at[h, a - 1], along(a, h)))
    for h in range(2):
        for k, term in enumerate(terms(0, h)):
            line[h, k] = term
    c_root.wait_recv()
    for src, dst in ((v_root, t_root), (v_root2, t_root2)):
        for k in range(4):
            for q in range(2):
                dst[pl.ds(k * BLOCK, BLOCK), pl.ds(q * BLOCK, BLOCK)] = src[
                    pl.ds(q * BLOCK, BLOCK), pl.ds(k * BLOCK, BLOCK)
                ].T
    for c in c3:
        c.wait_recv()
    sent_copies.extend(c3)
    c3 = []
    here = (my, mx)
    for h in range(2):
        for a in NEAR:
            k = lax.rem(here[h] + a, SIDE)
            total = line[h, k]
            for q in range(3):
                total = total + r3[h, q, k].astype(F32)
            u3[h, a - 1] = total.astype(BF16)
            c3.append(
                send(u3.at[h, a - 1], w3.at[h, a - 1], t3b.at[h, a - 1], m3b.at[h, a - 1], along(a, 1 - h))
            )
    for h in range(2):
        total = line[h, here[h]]
        for q in range(3):
            total = total + r3[h, q, here[h]].astype(F32)
        update[h] = total
    for c in c3:
        c.wait_recv()
    sent_copies.extend(c3)
    for h in range(2):
        total = update[h]
        for q in range(3):
            total = total + w3[h, q].astype(F32)
        update[h] = total
    update[2] = jnp.zeros((BLOCK, BLOCK), F32)

    picks = [root_map[0, 0, i] for i in range(2)]
    for q in range(4):
        idx = jnp.where(picks[0] == q, 0, jnp.where(picks[1] == q, 1, 2))
        s4[pl.ds(q * 2, 2)] = update[idx].reshape(2, CORES, SLICE, BLOCK)

    low = lax.broadcasted_iota(jnp.int32, (ROOT_ROWS, BLOCK), 1) < BLOCK // 2

    def turn(x):
        return pltpu.roll(x, BLOCK // 2, 1)

    def half_of(first, second, c):
        return jnp.where(low, jnp.where(c == 0, first, turn(first)), jnp.where(c == 0, turn(second), second))

    def side_by_side(first, second):
        return jnp.where(low, first, turn(second))

    def slices(x):
        return x.reshape(HALF_RING, SLICE, BLOCK)

    def flat(x):
        return x.reshape(ROOT_ROWS, BLOCK)

    def start_pair():
        first, second = flat(s4[:, 0]), flat(s4[:, 1])
        q4[...] = slices(half_of(first, second, 1 - gc).astype(BF16))
        c = send(q4, p4, pair_sems.at[0, 0], pair_sems.at[1, 0], (other, m))
        own = half_of(first, second, gc)
        c.wait_recv()
        sent_copies.append(c)
        u4[...] = slices((own + flat(p4[...]).astype(F32)).astype(BF16))

    def start_sum(u, r, k):
        for i, z in enumerate(chips):
            send(u.at[lax.rem(z, HALF_RING)], r.at[i], g_sems.at[0, k], g_sems.at[1, k], (z * CORES + gc, m))

    def finish_sum(u, r, k):
        drain(r, g_sems.at[1, k])
        total = u[gp].astype(F32)
        for i in range(len(chips)):
            total = total + r[i].astype(F32)
        sent.append((r, g_sems.at[0, k]))
        return total.astype(BF16)

    def start_gather(r, k):
        for z in half_ring:
            send(r.at[gp], r.at[gp], g_sems.at[0, k], g_sems.at[1, k], (z * CORES + gc, m))

    def finish_gather(r, k):
        seven = u4.at[: len(half_ring)]
        drain(seven, g_sems.at[1, k])
        sent.append((seven, g_sems.at[0, k]))

    start_pair()
    start_sum(u4, r4, 0)
    for k in range(PIVOT_BLOCKS):
        t_mid[pl.ds(k * BLOCK, BLOCK), :] = v_mid[:, pl.ds(k * BLOCK, BLOCK)].T
    b_root[gp] = finish_sum(u4, r4, 0)
    start_gather(b_root, 1)
    for k in range(BORDER // BLOCK):
        t_border[:, pl.ds(k * BLOCK, BLOCK)] = v_border[k // 8, k // 2 % 4, k % 2].T
    finish_gather(b_root, 1)

    b_even = flat(b_root[...]).astype(F32)
    b_rows = jnp.concatenate([slices(b_even), slices(turn(b_even))], axis=1)
    b_rows = b_rows.reshape(SHARE, BLOCK).astype(BF16)
    s5[...] = side_by_side(dot(v_root[...], b_rows), dot(v_root2[...], b_rows)).astype(BF16)
    c5 = []
    for i, d in enumerate(members):
        rows = pl.ds(pl.multiple_of(d * PIECE, PIECE), PIECE)
        c5.append(send(s5.at[rows], r5.at[i], send_sems.at[5], m5, (g, d)))
    sent.append((r5, send_sems.at[5]))
    drain(r5, m5)
    rows = pl.ds(pl.multiple_of(m * PIECE, PIECE), PIECE)
    acc = s5[rows, :].astype(F32)
    for i in range(len(members)):
        acc = acc + r5[i].astype(F32)
    s5b[...] = acc.astype(BF16)
    for i, d in enumerate(members):
        send(s5b, y_root.at[rows], send_sems.at[6], m5b, (g, d))
    y_root[rows, :] = s5b[...]
    sent.append((r5, send_sems.at[6]))
    drain(r5, m5b)

    y_own = y_root[...]
    y_other = turn(y_own.astype(F32)).astype(BF16)
    x_part = dot(t_root[...], y_own) + dot(t_root2[...], y_other)
    x_part = x_part.reshape(HALF_RING, CORES, SLICE, BLOCK)
    u6[...] = slices(side_by_side(flat(x_part[:, 0]), flat(x_part[:, 1])).astype(BF16))
    start_sum(u6, r6, 2)
    for k in range(LEAF // BLOCK):
        for q in range(EDGE // BLOCK):
            t_edge[pl.ds(k * BLOCK, BLOCK), pl.ds(q * BLOCK, BLOCK)] = v_edge[
                pl.ds(q * BLOCK, BLOCK), pl.ds(k * BLOCK, BLOCK)
            ].T
    x_half[gp] = finish_sum(u6, r6, 2)
    start_gather(x_half, 3)
    for k in range(LEAF // BLOCK):
        for q in range(k, LEAF // BLOCK):
            t_leaf[pl.ds(k * BLOCK, BLOCK), pl.ds(q * BLOCK, BLOCK)] = v_leaf[
                pl.ds(q * BLOCK, BLOCK), pl.ds(k * BLOCK, BLOCK)
            ].T
        for q in range(k - k % 2, k):
            t_leaf[pl.ds(k * BLOCK, BLOCK), pl.ds(q * BLOCK, BLOCK)] = v_leaf[
                pl.ds(q * BLOCK, BLOCK), pl.ds(k * BLOCK, BLOCK)
            ].T
    finish_gather(x_half, 3)
    c = send(x_half, x_other, pair_sems.at[0, 2], pair_sems.at[1, 2], (other, m))
    c.wait_recv()
    sent_copies.append(c)
    mine, theirs = flat(x_half[...]).astype(F32), flat(x_other[...]).astype(F32)
    left, right = jnp.where(gc == 0, mine, theirs), jnp.where(gc == 0, theirs, mine)
    x_root[:, 0] = slices(jnp.where(low, left, turn(right)).astype(BF16))
    x_root[:, 1] = slices(jnp.where(low, turn(left), right).astype(BF16))
    x_blocks[...] = x_root[...].reshape(4, BLOCK, BLOCK)
    out_rows = pl.ds(pl.multiple_of(lax.rem(g, 2) * PIECE, PIECE), PIECE)
    root_o[0] = x_root[g // 4, lax.rem(g // 2, 2), out_rows]

    for h in range(2):
        front[PIVOT_BLOCKS + 2 * m + h] = x_blocks[picks[h]]

    def forward_block(a, b, h, to):
        k = PIVOT_BLOCKS + 2 * member_at((SIDE - a) % SIDE, (SIDE - b) % SIDE) + h
        a2, b2 = a + to[0], b + to[1]
        c = send(front.at[k], front.at[k], t7.at[h, a2, b2], m7.at[h, a2, b2], (g, member_at(*to)))
        sent_copies.append(c)
        return c

    c7 = {}
    for a in NEAR:
        c7[0, a, 0] = forward_block(0, 0, 0, (a, 0))
        c7[1, 0, a] = forward_block(0, 0, 1, (0, a))
    for a in NEAR:
        c7[0, 0, a] = forward_block(0, 0, 0, (0, a))
        c7[1, a, 0] = forward_block(0, 0, 1, (a, 0))
    for a in (1, 3, 2):
        c7.pop((0, a, 0)).wait_recv()
        for b in NEAR:
            c7[0, a, b] = forward_block(a, 0, 0, (0, b))
        c7.pop((1, 0, a)).wait_recv()
        for b in NEAR:
            c7[1, b, a] = forward_block(0, a, 1, (b, 0))
    for c in c7.values():
        c.wait_recv()
    back = dot(t_border[...], front[PIVOT_BLOCKS:].reshape(BORDER, BLOCK))
    mid_back[...] = (mid_forward[...].astype(F32) - back).astype(BF16)

    c8 = []
    for d in range(MEMBERS):
        c8.append(copy_to(s8.at[d], r8.at[m], t8.at[d], m8.at[m], (g, d)))
    for q in range(SIDE):

        @pl.when(q <= mx)
        def _(q=q):
            product = dot(t_mid[pl.ds(q * SHARE, SHARE), :], mid_back[...])
            s8[pl.ds(q * SIDE, SIDE)] = product.astype(BF16).reshape(SIDE, BLOCK, BLOCK)
            for d in range(q * SIDE, (q + 1) * SIDE):
                pl.when(d < m)(c8[d].start)

    for d in range(MEMBERS):
        partial_sends.append((d < m, c8[d]))
    total = s8[m].astype(F32)
    for d in range(MEMBERS):
        c = copy_to(s8.at[d], r8.at[d], t8.at[d], m8.at[d], (g, d))
        pl.when(d > m)(c.wait_recv)
        total = total + r8[d].astype(F32)
    front[m] = total.astype(BF16)
    mid_o[0] = total.astype(BF16)
    c8b = []
    for i, d in enumerate(members):
        c8b.append(send(front.at[m], front.at[m], send_sems.at[11], m8b.at[i], (g, d)))
    sent.append((s1, send_sems.at[11]))
    for c in c8b:
        c.wait_recv()

    lb = forward[...].astype(F32)
    for j in range(LEAF_BLOCKS):
        lb = lb - dot(t_edge[:, pl.ds(j * BLOCK, BLOCK)], front[targets[j]])
    lb = lb.astype(BF16)
    for i in range(3):
        leaf_o[0, 0, pl.ds(i * 256, 256), :] = dot(
            t_leaf[pl.ds(i * 256, 256), i * 256 :], lb[i * 256 :]
        ).astype(BF16)

    finish()


def write_out(*refs):
    for src, dst in zip(refs[:3], refs[3:]):
        dst[...] = src[...]


def on_device(rhs, leaf_inverse, leaf_edge, leaf_map, mid_inverse, mid_border, *rest):
    blocks = mid_border.reshape(1, SIDE, SIDE, 2, BLOCK, BLOCK)
    args = (rhs, leaf_inverse, leaf_edge, jnp.swapaxes(leaf_map, 1, 2), mid_inverse, blocks, *rest)
    n_m, n_z = MEMBERS - 1, CHIPS - 1
    piece = (PIECE, BLOCK)
    part = (SLICE, BLOCK)
    dma = pltpu.SemaphoreType.DMA
    block = (BLOCK, BLOCK)
    v = lambda *shape: pltpu.VMEM(shape, BF16)
    scratch = [
        v(LEAF, BLOCK),
        v(LEAF, LEAF),
        v(EDGE, LEAF),
        v(BLOCK, PIVOTS),
        v(SIDE, SIDE, 2, *block),
        v(ROOT_ROWS, SHARE),
        v(ROOT_ROWS, SHARE),
        v(LEAF, LEAF),
        v(LEAF, EDGE),
        v(PIVOTS, BLOCK),
        v(BLOCK, BORDER),
        v(SHARE, ROOT_ROWS),
        v(SHARE, ROOT_ROWS),
        v(LEAF, BLOCK),
        v(LEAF_BLOCKS + 1, *block),
        v(n_m, *block),
        v(n_m, *block),
        v(*block),
        v(MEMBERS, *block),
        v(*block),
        v(2, 3, SIDE, *block),
        v(2, 3, SIDE, *block),
        pltpu.VMEM((2, SIDE, *block), F32),
        v(2, 3, *block),
        v(2, 3, *block),
        pltpu.VMEM((3, *block), F32),
        pltpu.VMEM((HALF_RING, CORES, *part), F32),
        v(HALF_RING, *part),
        v(HALF_RING, *part),
        v(HALF_RING, *part),
        v(n_z, *part),
        v(HALF_RING, *part),
        v(ROOT_ROWS, BLOCK),
        v(n_m, *piece),
        v(*piece),
        v(ROOT_ROWS, BLOCK),
        v(HALF_RING, *part),
        v(n_z, *part),
        v(HALF_RING, *part),
        v(HALF_RING, *part),
        v(HALF_RING, CORES, *part),
        v(4, *block),
        v(FRONT_BLOCKS, *block),
        v(*block),
        v(MEMBERS, *block),
        v(MEMBERS, *block),
        dma((6,)),
        dma((12,)),
        dma((n_m,)),
        dma((n_m,)),
        dma((n_m,)),
        dma((2, 3)),
        dma((2, 3)),
        dma((2, 3)),
        dma((2, 3)),
        dma,
        dma,
        dma((2, SIDE, SIDE)),
        dma((2, SIDE, SIDE)),
        dma((MEMBERS,)),
        dma((MEMBERS,)),
        dma((n_m,)),
        dma((2, 4)),
        dma((2, 4)),
    ]
    anywhere = pl.BlockSpec(memory_space=pltpu.HBM)
    scalars = pl.BlockSpec(memory_space=pltpu.SMEM)
    vmem = pl.BlockSpec(memory_space=pltpu.VMEM)
    shapes = (
            jax.ShapeDtypeStruct((1, 1, LEAF, BLOCK), BF16),
            jax.ShapeDtypeStruct((1, BLOCK, BLOCK), BF16),
            jax.ShapeDtypeStruct((1, PIECE, BLOCK), BF16),
    )
    values = pl.pallas_call(
        whole_kernel,
        out_shape=shapes,
        in_specs=[anywhere, anywhere, anywhere, scalars, anywhere, anywhere, scalars, anywhere],
        out_specs=(vmem, vmem, vmem),
        scratch_shapes=scratch,
        name="solve",
        compiler_params=pltpu.CompilerParams(
            collective_id=0, has_side_effects=True, vmem_limit_bytes=63_000_000
        ),
    )(*args)
    return pl.pallas_call(
        write_out,
        out_shape=shapes,
        in_specs=[vmem] * 3,
        out_specs=(vmem,) * 3,
        name="write",
    )(*values)


def solution(mesh):
    in_specs = (
        P("group", "member", None, None),
        P("group", "member", None, None),
        P("group", "member", None, None),
        P("group", None, None),
        P("group", "member", None),
        P("group", None, "member"),
        P("group", "member", None),
        P("group", "member"),
    )
    out_specs = (
        P("group", "member", None, None),
        P("group", "member", None),
        P("member", "group", None),
    )
    return jax.shard_map(
        on_device, mesh=mesh, in_specs=in_specs, out_specs=out_specs, check_vma=False
    )
```

```python
import functools

import jax
import jax.numpy as jnp
from jax import lax
from jax.experimental import pallas as pl
from jax.experimental.pallas import tpu as pltpu
from jax.sharding import PartitionSpec as P

BLOCK = 128
SIDE = 4
MEMBERS = 16
CORES = 2
CHIPS = 16
LEAF = 768
EDGE = 512
LEAF_BLOCKS = EDGE // BLOCK
PIVOTS = 2048
PIVOT_BLOCKS = PIVOTS // BLOCK
BORDER = 4096
FRONT_BLOCKS = (PIVOTS + BORDER) // BLOCK
SHARE = 512
ROOT_ROWS = 256
PIECE = 16
MESH = pl.DeviceIdType.MESH
F32 = jnp.float32
BF16 = jnp.bfloat16

MEMBER_OFFSETS = [
    (2, 2),
    (2, 1),
    (1, 2),
    (2, 3),
    (3, 2),
    (1, 1),
    (3, 3),
    (1, 3),
    (3, 1),
    (2, 0),
    (0, 2),
    (1, 0),
    (3, 0),
    (0, 1),
    (0, 3),
]
CHIP_OFFSETS = sorted(range(1, CHIPS), key=lambda a: -min(a, CHIPS - a))
HALF_RING = CHIPS // 2
HALF_OFFSETS = (4, 3, 13, 2, 14, 1, 15)
SLICE = 32
NEAR = (1, 3, 2)


def dot(a, b):
    return jnp.dot(a, b, preferred_element_type=F32)


def whole_kernel(
    rhs,
    leaf_inverse,
    leaf_edge,
    leaf_map,
    mid_inverse,
    mid_border,
    root_map,
    root_inverse,
    leaf_o,
    mid_o,
    root_o,
    v_rhs,
    v_leaf,
    v_edge,
    v_mid,
    v_border,
    v_root,
    v_root2,
    t_leaf,
    t_edge,
    t_mid,
    t_border,
    t_root,
    t_root2,
    forward,
    leaf_out,
    s1,
    r1,
    s2,
    r2,
    mid_forward,
    s3,
    r3,
    line,
    u3,
    w3,
    update,
    s4,
    q4,
    p4,
    u4,
    r4,
    b_root,
    s5,
    r5,
    s5b,
    y_root,
    u6,
    r6,
    x_half,
    x_other,
    x_root,
    x_blocks,
    front,
    mid_back,
    s8,
    r8,
    load_sems,
    send_sems,
    m1,
    t2,
    m2,
    t3,
    m3,
    t3b,
    m3b,
    m5,
    m5b,
    t7,
    m7,
    t8,
    m8,
    m8b,
    g_sems,
    pair_sems,
):
    g = lax.axis_index("group")
    m = lax.axis_index("member")
    mx, my = m // SIDE, lax.rem(m, SIDE)
    gz, gc = g // CORES, lax.rem(g, CORES)
    other = gz * CORES + 1 - gc

    def member_at(a, b):
        return lax.rem(mx + a, SIDE) * SIDE + lax.rem(my + b, SIDE)

    members, sources = [], []
    for a, b in MEMBER_OFFSETS:
        up, down = member_at(a, b), member_at((SIDE - a) % SIDE, (SIDE - b) % SIDE)
        members.append(jnp.where(gc == 0, up, down))
        sources.append(jnp.where(gc == 0, down, up))
    chips = [lax.rem(gz + a, CHIPS) for a in CHIP_OFFSETS]
    half_ring = [
        lax.rem(gz + jnp.where(gc == 0, a, CHIPS - a), CHIPS) for a in HALF_OFFSETS
    ]
    gp = lax.rem(gz, HALF_RING)

    barrier = pltpu.get_barrier_semaphore()
    for z in chips:
        pl.semaphore_signal(barrier, inc=1, device_id=(z * CORES + gc, m), device_id_type=MESH)
    pl.semaphore_signal(barrier, inc=1, device_id=(other, m), device_id_type=MESH)
    for d in members:
        pl.semaphore_signal(barrier, inc=1, device_id=(g, d), device_id_type=MESH)

    loads = []
    for i, (src, dst) in enumerate(
        [
            (rhs.at[0, 0], v_rhs),
            (leaf_inverse.at[0, 0], v_leaf),
            (leaf_edge.at[0, 0], v_edge),
            (root_inverse, v_root),
            (mid_inverse.at[0], v_mid),
            (mid_border.at[0], v_border),
        ]
    ):
        c = pltpu.make_async_copy(src, dst, load_sems.at[i])
        c.start()
        loads.append(c)

    def copy_to(src, dst, ssem, rsem, device):
        return pltpu.make_async_remote_copy(
            src_ref=src,
            dst_ref=dst,
            send_sem=ssem,
            recv_sem=rsem,
            device_id=device,
            device_id_type=MESH,
        )

    def send(*args):
        c = copy_to(*args)
        c.start()
        return c

    def drain(ref, sem):
        pltpu.make_async_copy(ref, ref, sem).wait()

    sent = []
    partial_sends = []
    sent_copies = []
    pending = list(loads)

    def loaded(n):
        for _ in range(n):
            pending.pop(0).wait()

    def finish():
        loaded(len(pending))
        for ref, i in sent:
            drain(ref, i)
        for when, c in partial_sends:
            pl.when(when)(c.wait_send)
        for c in sent_copies:
            c.wait_send()

    targets = [leaf_map[0, j, m] for j in range(LEAF_BLOCKS)]

    def leaf_block(k):
        idx = jnp.int32(LEAF_BLOCKS)
        for j in range(LEAF_BLOCKS):
            idx = jnp.where(targets[j] == k, j, idx)
        return leaf_out[idx]

    leaf_out[LEAF_BLOCKS] = jnp.zeros((BLOCK, BLOCK), BF16)
    r2[...] = jnp.zeros_like(r2)
    r8[...] = jnp.zeros_like(r8)
    loaded(2)
    for i in range(3):
        rows = pl.ds(i * 256, 256)
        depth = (i + 1) * 256
        forward[rows, :] = dot(v_leaf[rows, :depth], v_rhs[:depth, :]).astype(BF16)
    loaded(1)
    for j in range(LEAF_BLOCKS):
        leaf_out[j] = (-dot(v_edge[pl.ds(j * BLOCK, BLOCK), :], forward[...])).astype(BF16)

    pl.semaphore_wait(barrier, len(chips) + 1 + len(members))

    loaded(1)
    c_root = send(v_root, v_root2, pair_sems.at[0, 1], pair_sems.at[1, 1], (other, m))
    sent_copies.append(c_root)
    c1 = []
    for i, d in enumerate(members):
        s1[i] = leaf_block(d)
        c1.append(send(s1.at[i], r1.at[i], send_sems.at[0], m1.at[i], (g, d)))
    loaded(2)
    sent.append((s1, send_sems.at[0]))
    total = leaf_block(m).astype(F32)
    for i, c in enumerate(c1):
        c.wait_recv()
        total = total + r1[i].astype(F32)
    s2[...] = total.astype(BF16)
    c2 = []
    for i, d in enumerate(members):
        c = copy_to(s2, r2.at[m], t2.at[i], m2.at[i], (g, d))
        pl.when(d > m)(c.start)
        partial_sends.append((d > m, c))
        c2.append(c)
    r2[m] = s2[...]
    for i, c in enumerate(c2):
        pl.when(sources[i] < m)(c.wait_recv)
    mf = dot(v_mid[...], r2[...].reshape(PIVOTS, BLOCK)).astype(BF16)
    mid_forward[...] = mf

    def terms(a, h):
        at = lax.rem((mx, my)[h] + a, SIDE)
        rows = v_border[at, :, h] if h == 0 else v_border[:, at, h]
        product = dot(rows.reshape(SIDE * BLOCK, BLOCK), mid_forward[...])
        out = []
        for k in range(SIDE):
            d = at * SIDE + k if h == 0 else k * SIDE + at
            out.append(
                leaf_block(PIVOT_BLOCKS + 2 * d + h).astype(F32) - product[k * BLOCK : (k + 1) * BLOCK]
            )
        return out

    def along(a, h):
        return (g, member_at(a, 0) if h == 0 else member_at(0, a))

    c3 = []
    for a in NEAR:
        for h in range(2):
            for k, term in enumerate(terms(a, h)):
                s3[h, a - 1, k] = term.astype(BF16)
            c3.append(send(s3.at[h, a - 1], r3.at[h, a - 1], t3.at[h, a - 1], m3.at[h, a - 1], along(a, h)))
    for h in range(2):
        for k, term in enumerate(terms(0, h)):
            line[h, k] = term
    c_root.wait_recv()
    for src, dst in ((v_root, t_root), (v_root2, t_root2)):
        for k in range(4):
            for q in range(2):
                dst[pl.ds(k * BLOCK, BLOCK), pl.ds(q * BLOCK, BLOCK)] = src[
                    pl.ds(q * BLOCK, BLOCK), pl.ds(k * BLOCK, BLOCK)
                ].T
    for c in c3:
        c.wait_recv()
    sent_copies.extend(c3)
    c3 = []
    here = (my, mx)
    for h in range(2):
        for a in NEAR:
            k = lax.rem(here[h] + a, SIDE)
            total = line[h, k]
            for q in range(3):
                total = total + r3[h, q, k].astype(F32)
            u3[h, a - 1] = total.astype(BF16)
            c3.append(
                send(u3.at[h, a - 1], w3.at[h, a - 1], t3b.at[h, a - 1], m3b.at[h, a - 1], along(a, 1 - h))
            )
    for h in range(2):
        total = line[h, here[h]]
        for q in range(3):
            total = total + r3[h, q, here[h]].astype(F32)
        update[h] = total
    for c in c3:
        c.wait_recv()
    sent_copies.extend(c3)
    for h in range(2):
        total = update[h]
        for q in range(3):
            total = total + w3[h, q].astype(F32)
        update[h] = total
    update[2] = jnp.zeros((BLOCK, BLOCK), F32)

    picks = [root_map[0, 0, i] for i in range(2)]
    for q in range(4):
        idx = jnp.where(picks[0] == q, 0, jnp.where(picks[1] == q, 1, 2))
        s4[pl.ds(q * 2, 2)] = update[idx].reshape(2, CORES, SLICE, BLOCK)

    low = lax.broadcasted_iota(jnp.int32, (ROOT_ROWS, BLOCK), 1) < BLOCK // 2

    def turn(x):
        return pltpu.roll(x, BLOCK // 2, 1)

    def half_of(first, second, c):
        return jnp.where(low, jnp.where(c == 0, first, turn(first)), jnp.where(c == 0, turn(second), second))

    def side_by_side(first, second):
        return jnp.where(low, first, turn(second))

    def slices(x):
        return x.reshape(HALF_RING, SLICE, BLOCK)

    def flat(x):
        return x.reshape(ROOT_ROWS, BLOCK)

    def start_pair():
        first, second = flat(s4[:, 0]), flat(s4[:, 1])
        q4[...] = slices(half_of(first, second, 1 - gc).astype(BF16))
        c = send(q4, p4, pair_sems.at[0, 0], pair_sems.at[1, 0], (other, m))
        own = half_of(first, second, gc)
        c.wait_recv()
        sent_copies.append(c)
        u4[...] = slices((own + flat(p4[...]).astype(F32)).astype(BF16))

    def start_sum(u, r, k):
        for i, z in enumerate(chips):
            send(u.at[lax.rem(z, HALF_RING)], r.at[i], g_sems.at[0, k], g_sems.at[1, k], (z * CORES + gc, m))

    def finish_sum(u, r, k):
        drain(r, g_sems.at[1, k])
        total = u[gp].astype(F32)
        for i in range(len(chips)):
            total = total + r[i].astype(F32)
        sent.append((r, g_sems.at[0, k]))
        return total.astype(BF16)

    def start_gather(r, k):
        for z in half_ring:
            send(r.at[gp], r.at[gp], g_sems.at[0, k], g_sems.at[1, k], (z * CORES + gc, m))

    def finish_gather(r, k):
        seven = u4.at[: len(half_ring)]
        drain(seven, g_sems.at[1, k])
        sent.append((seven, g_sems.at[0, k]))

    start_pair()
    start_sum(u4, r4, 0)
    for k in range(PIVOT_BLOCKS):
        t_mid[pl.ds(k * BLOCK, BLOCK), :] = v_mid[:, pl.ds(k * BLOCK, BLOCK)].T
    b_root[gp] = finish_sum(u4, r4, 0)
    start_gather(b_root, 1)
    for k in range(BORDER // BLOCK):
        t_border[k // 2, :, pl.ds(k % 2 * BLOCK, BLOCK)] = v_border[k // 8, k // 2 % 4, k % 2].T
    finish_gather(b_root, 1)

    b_even = flat(b_root[...]).astype(F32)
    b_rows = jnp.concatenate([slices(b_even), slices(turn(b_even))], axis=1)
    b_rows = b_rows.reshape(SHARE, BLOCK).astype(BF16)
    s5[...] = side_by_side(dot(v_root[...], b_rows), dot(v_root2[...], b_rows)).astype(BF16)
    c5 = []
    for i, d in enumerate(members):
        rows = pl.ds(pl.multiple_of(d * PIECE, PIECE), PIECE)
        c5.append(send(s5.at[rows], r5.at[i], send_sems.at[5], m5, (g, d)))
    sent.append((r5, send_sems.at[5]))
    drain(r5, m5)
    rows = pl.ds(pl.multiple_of(m * PIECE, PIECE), PIECE)
    acc = s5[rows, :].astype(F32)
    for i in range(len(members)):
        acc = acc + r5[i].astype(F32)
    s5b[...] = acc.astype(BF16)
    for i, d in enumerate(members):
        send(s5b, y_root.at[rows], send_sems.at[6], m5b, (g, d))
    y_root[rows, :] = s5b[...]
    sent.append((r5, send_sems.at[6]))
    drain(r5, m5b)

    y_own = y_root[...]
    y_other = turn(y_own.astype(F32)).astype(BF16)
    x_part = dot(t_root[...], y_own) + dot(t_root2[...], y_other)
    x_part = x_part.reshape(HALF_RING, CORES, SLICE, BLOCK)
    u6[...] = slices(side_by_side(flat(x_part[:, 0]), flat(x_part[:, 1])).astype(BF16))
    start_sum(u6, r6, 2)
    for k in range(LEAF // BLOCK):
        for q in range(EDGE // BLOCK):
            t_edge[pl.ds(k * BLOCK, BLOCK), pl.ds(q * BLOCK, BLOCK)] = v_edge[
                pl.ds(q * BLOCK, BLOCK), pl.ds(k * BLOCK, BLOCK)
            ].T
    x_half[gp] = finish_sum(u6, r6, 2)
    start_gather(x_half, 3)
    for k in range(LEAF // BLOCK):
        for q in range(k, LEAF // BLOCK):
            t_leaf[pl.ds(k * BLOCK, BLOCK), pl.ds(q * BLOCK, BLOCK)] = v_leaf[
                pl.ds(q * BLOCK, BLOCK), pl.ds(k * BLOCK, BLOCK)
            ].T
        for q in range(k - k % 2, k):
            t_leaf[pl.ds(k * BLOCK, BLOCK), pl.ds(q * BLOCK, BLOCK)] = v_leaf[
                pl.ds(q * BLOCK, BLOCK), pl.ds(k * BLOCK, BLOCK)
            ].T
    finish_gather(x_half, 3)
    c = send(x_half, x_other, pair_sems.at[0, 2], pair_sems.at[1, 2], (other, m))
    c.wait_recv()
    sent_copies.append(c)
    mine, theirs = flat(x_half[...]).astype(F32), flat(x_other[...]).astype(F32)
    left, right = jnp.where(gc == 0, mine, theirs), jnp.where(gc == 0, theirs, mine)
    x_root[:, 0] = slices(jnp.where(low, left, turn(right)).astype(BF16))
    x_root[:, 1] = slices(jnp.where(low, turn(left), right).astype(BF16))
    x_blocks[...] = x_root[...].reshape(4, BLOCK, BLOCK)
    out_rows = pl.ds(pl.multiple_of(lax.rem(g, 2) * PIECE, PIECE), PIECE)
    root_o[0] = x_root[g // 4, lax.rem(g // 2, 2), out_rows]

    for h in range(2):
        front[PIVOT_BLOCKS + 2 * m + h] = x_blocks[picks[h]]

    def forward_block(a, b, h, to):
        k = PIVOT_BLOCKS + 2 * member_at((SIDE - a) % SIDE, (SIDE - b) % SIDE) + h
        a2, b2 = a + to[0], b + to[1]
        c = send(front.at[k], front.at[k], t7.at[h, a2, b2], m7.at[h, a2, b2], (g, member_at(*to)))
        sent_copies.append(c)
        return c

    c7 = {}
    for a in NEAR:
        c7[0, a, 0] = forward_block(0, 0, 0, (a, 0))
        c7[1, 0, a] = forward_block(0, 0, 1, (0, a))
    for a in NEAR:
        c7[0, 0, a] = forward_block(0, 0, 0, (0, a))
        c7[1, a, 0] = forward_block(0, 0, 1, (a, 0))
    for a in (1, 3, 2):
        c7.pop((0, a, 0)).wait_recv()
        for b in NEAR:
            c7[0, a, b] = forward_block(a, 0, 0, (0, b))
        c7.pop((1, 0, a)).wait_recv()
        for b in NEAR:
            c7[1, b, a] = forward_block(0, a, 1, (b, 0))
    order = [(0, 0)] + [(a, 0) for a in NEAR] + [(0, a) for a in NEAR]
    order += [(a, b) for a in (1, 3, 2) for b in (1, 3, 2)]
    back = mid_forward[...].astype(F32)
    for a, b in order:
        for h in range(2):
            if (h, a, b) in c7:
                c7[h, a, b].wait_recv()
        d = member_at((SIDE - a) % SIDE, (SIDE - b) % SIDE)
        values = front[pl.ds(PIVOT_BLOCKS + 2 * d, 2)].reshape(2 * BLOCK, BLOCK)
        back = back - dot(t_border[d], values)
    mid_back[...] = back.astype(BF16)

    c8 = []
    for d in range(MEMBERS):
        c8.append(copy_to(s8.at[d], r8.at[m], t8.at[d], m8.at[m], (g, d)))
    for q in range(SIDE):

        @pl.when(q <= mx)
        def _(q=q):
            product = dot(t_mid[pl.ds(q * SHARE, SHARE), :], mid_back[...])
            s8[pl.ds(q * SIDE, SIDE)] = product.astype(BF16).reshape(SIDE, BLOCK, BLOCK)
            for d in range(q * SIDE, (q + 1) * SIDE):
                pl.when(d < m)(c8[d].start)

    for d in range(MEMBERS):
        partial_sends.append((d < m, c8[d]))
    total = s8[m].astype(F32)
    for d in range(MEMBERS):
        c = copy_to(s8.at[d], r8.at[d], t8.at[d], m8.at[d], (g, d))
        pl.when(d > m)(c.wait_recv)
        total = total + r8[d].astype(F32)
    front[m] = total.astype(BF16)
    mid_o[0] = total.astype(BF16)
    c8b = []
    for i, d in enumerate(members):
        c8b.append(send(front.at[m], front.at[m], send_sems.at[11], m8b.at[i], (g, d)))
    sent.append((s1, send_sems.at[11]))
    for c in c8b:
        c.wait_recv()

    lb = forward[...].astype(F32)
    for j in range(LEAF_BLOCKS):
        lb = lb - dot(t_edge[:, pl.ds(j * BLOCK, BLOCK)], front[targets[j]])
    lb = lb.astype(BF16)
    for i in range(3):
        leaf_o[0, 0, pl.ds(i * 256, 256), :] = dot(
            t_leaf[pl.ds(i * 256, 256), i * 256 :], lb[i * 256 :]
        ).astype(BF16)

    finish()


def write_out(*refs):
    for src, dst in zip(refs[:3], refs[3:]):
        dst[...] = src[...]


def on_device(rhs, leaf_inverse, leaf_edge, leaf_map, mid_inverse, mid_border, *rest):
    blocks = mid_border.reshape(1, SIDE, SIDE, 2, BLOCK, BLOCK)
    args = (rhs, leaf_inverse, leaf_edge, jnp.swapaxes(leaf_map, 1, 2), mid_inverse, blocks, *rest)
    n_m, n_z = MEMBERS - 1, CHIPS - 1
    piece = (PIECE, BLOCK)
    part = (SLICE, BLOCK)
    dma = pltpu.SemaphoreType.DMA
    block = (BLOCK, BLOCK)
    v = lambda *shape: pltpu.VMEM(shape, BF16)
    scratch = [
        v(LEAF, BLOCK),
        v(LEAF, LEAF),
        v(EDGE, LEAF),
        v(BLOCK, PIVOTS),
        v(SIDE, SIDE, 2, *block),
        v(ROOT_ROWS, SHARE),
        v(ROOT_ROWS, SHARE),
        v(LEAF, LEAF),
        v(LEAF, EDGE),
        v(PIVOTS, BLOCK),
        v(MEMBERS, BLOCK, 2 * BLOCK),
        v(SHARE, ROOT_ROWS),
        v(SHARE, ROOT_ROWS),
        v(LEAF, BLOCK),
        v(LEAF_BLOCKS + 1, *block),
        v(n_m, *block),
        v(n_m, *block),
        v(*block),
        v(MEMBERS, *block),
        v(*block),
        v(2, 3, SIDE, *block),
        v(2, 3, SIDE, *block),
        pltpu.VMEM((2, SIDE, *block), F32),
        v(2, 3, *block),
        v(2, 3, *block),
        pltpu.VMEM((3, *block), F32),
        pltpu.VMEM((HALF_RING, CORES, *part), F32),
        v(HALF_RING, *part),
        v(HALF_RING, *part),
        v(HALF_RING, *part),
        v(n_z, *part),
        v(HALF_RING, *part),
        v(ROOT_ROWS, BLOCK),
        v(n_m, *piece),
        v(*piece),
        v(ROOT_ROWS, BLOCK),
        v(HALF_RING, *part),
        v(n_z, *part),
        v(HALF_RING, *part),
        v(HALF_RING, *part),
        v(HALF_RING, CORES, *part),
        v(4, *block),
        v(FRONT_BLOCKS, *block),
        v(*block),
        v(MEMBERS, *block),
        v(MEMBERS, *block),
        dma((6,)),
        dma((12,)),
        dma((n_m,)),
        dma((n_m,)),
        dma((n_m,)),
        dma((2, 3)),
        dma((2, 3)),
        dma((2, 3)),
        dma((2, 3)),
        dma,
        dma,
        dma((2, SIDE, SIDE)),
        dma((2, SIDE, SIDE)),
        dma((MEMBERS,)),
        dma((MEMBERS,)),
        dma((n_m,)),
        dma((2, 4)),
        dma((2, 4)),
    ]
    anywhere = pl.BlockSpec(memory_space=pltpu.HBM)
    scalars = pl.BlockSpec(memory_space=pltpu.SMEM)
    vmem = pl.BlockSpec(memory_space=pltpu.VMEM)
    shapes = (
            jax.ShapeDtypeStruct((1, 1, LEAF, BLOCK), BF16),
            jax.ShapeDtypeStruct((1, BLOCK, BLOCK), BF16),
            jax.ShapeDtypeStruct((1, PIECE, BLOCK), BF16),
    )
    values = pl.pallas_call(
        whole_kernel,
        out_shape=shapes,
        in_specs=[anywhere, anywhere, anywhere, scalars, anywhere, anywhere, scalars, anywhere],
        out_specs=(vmem, vmem, vmem),
        scratch_shapes=scratch,
        name="solve",
        compiler_params=pltpu.CompilerParams(
            collective_id=0, has_side_effects=True, vmem_limit_bytes=63_000_000
        ),
    )(*args)
    return pl.pallas_call(
        write_out,
        out_shape=shapes,
        in_specs=[vmem] * 3,
        out_specs=(vmem,) * 3,
        name="write",
    )(*values)


def solution(mesh):
    in_specs = (
        P("group", "member", None, None),
        P("group", "member", None, None),
        P("group", "member", None, None),
        P("group", None, None),
        P("group", "member", None),
        P("group", None, "member"),
        P("group", "member", None),
        P("group", "member"),
    )
    out_specs = (
        P("group", "member", None, None),
        P("group", "member", None),
        P("member", "group", None),
    )
    return jax.shard_map(
        on_device, mesh=mesh, in_specs=in_specs, out_specs=out_specs, check_vma=False
    )
```
